256 devices in a mesh: dp: 8 (over y, core), expert: 32 (over x, z).
Axes of the slice: x: 4, y: 4, z: 8, core: 2. Of those that a mesh axis runs over, the one named last changes fastest.
Arguments:
- tokens: bfloat16 [32768, 1024], P(('dp', 'expert')), may hold values from -6 to 6
- expert_ids: int32 [32768, 8], P(('dp', 'expert')), may hold values from 0 to 31, as said below
- route_num: int32 [32768, 8], P(('dp', 'expert')), may hold values from 1 to 256
- w_gate: bfloat16 [32, 1024, 384], P('expert'), may hold values from -0.1875 to 0.1875
- w_up: bfloat16 [32, 1024, 384], P('expert'), may hold values from -0.1875 to 0.1875
- w_down: bfloat16 [32, 384, 1024], P('expert'), may hold values from -0.3125 to 0.3125
- cotangent: bfloat16 [32768, 1024], P(('dp', 'expert')), may hold values from -1.1953125 to 1.1953125
Outputs:
- output: bfloat16 [32768, 1024], P(('dp', 'expert'))
- tokens_grad: bfloat16 [32768, 1024], P(('dp', 'expert'))
- w_gate_grad: bfloat16 [32, 1024, 384], P('expert', 'dp')
- w_up_grad: bfloat16 [32, 1024, 384], P('expert', 'dp')
- w_down_grad: bfloat16 [32, 384, 1024], P('expert', None, 'dp')
The draws below stay inside these ranges and needn't reach their ends.
Inputs may be any that keep to these rules, and one draw needn't show every extreme that they name: `expert_ids`: each row names 8 different experts. Rows come in aligned blocks of 128, one device's tokens each, and 32 consecutive blocks form one data group. In each data group one expert is named by exactly 40 rows of every block of that group, and in no block is any expert named by more than 40 rows.
All inputs are finite; a program needn't handle non-finite values.
Results may differ from the reference program's by a relative error of at most 0.017.
Values may be sent and summed in bfloat16 or wider, within the bound.
No kernel may reach another device: no remote copies, remote signals or barrier semaphores. Data moves between devices by JAX's collectives and lax.ppermute only.
A program may use at most 128 MiB of HBM per device.

```python
import jax
import jax.numpy as jnp
from jax import lax

D = 1024
FF = 384
TOP = 8
DENOM = 256
TOK_DEV = 128
CAP = 40
RANKS = 32
EXPERTS = 32
TOKENS = 32768


def draw_expert_ids(key, part):
    key = jax.random.fold_in(key, 11)
    block_count = TOKENS // TOK_DEV
    other_picks = TOK_DEV * TOP - CAP
    span_low = max(2 * TOP, (other_picks + CAP - 1) // CAP)

    def one_block(block_idx):
        group_idx = block_idx // RANKS
        group_key = jax.random.fold_in(jax.random.fold_in(key, 7), group_idx)
        block_key = jax.random.fold_in(key, block_idx)
        hot_expert = jax.random.randint(group_key, (), 0, EXPERTS)
        key_order, key_rows, key_span, key_turn = jax.random.split(block_key, 4)
        row_order = jax.random.permutation(key_order, TOK_DEV)
        hot_row = (row_order < CAP).astype(jnp.int32)
        other_experts = jax.random.permutation(key_rows, EXPERTS - 1)
        other_experts = jnp.where(other_experts >= hot_expert, other_experts + 1, other_experts)
        span_len = jax.random.randint(key_span, (), span_low, EXPERTS)
        need_count = TOP - hot_row
        start_pos = jnp.cumsum(need_count) - need_count
        slot_pos = jnp.arange(TOP, dtype=jnp.int32)
        cycle_pos = jnp.mod(start_pos[:, None] + slot_pos[None, :] - hot_row[:, None], span_len)
        chosen = other_experts[cycle_pos]
        chosen = jnp.where((hot_row[:, None] == 1) & (slot_pos[None, :] == 0), hot_expert, chosen)
        rotation = jax.random.randint(key_turn, (TOK_DEV, 1), 0, TOP)
        columns = jnp.mod(slot_pos[None, :] + rotation, TOP)
        return jnp.take_along_axis(chosen, columns, axis=1)
    expert_table = jax.vmap(one_block)(jnp.arange(block_count, dtype=jnp.int32))
    return expert_table.reshape(TOKENS, TOP).astype(jnp.int32)


def touch_ends(array, stream_key, least, high):
    place = [jax.random.randint(jax.random.fold_in(stream_key, axis), (), 0, length) for axis, length in enumerate(array.shape)]
    longest = array.shape.index(max(array.shape))
    next_to = place[:longest] + [(place[longest] + 1) % array.shape[longest]] + place[longest + 1:]
    return array.at[tuple(place)].set(least).at[tuple(next_to)].set(high)


def shard_levels(stream_key, extent, cuts, smallest, top_value):
    factor_of = 1.0
    for dim, blocks in cuts:
        draws = jax.random.uniform(jax.random.fold_in(jax.random.fold_in(stream_key, 6), dim), (blocks,), jnp.float32, smallest / len(cuts), top_value / len(cuts))
        factor_of = factor_of * jnp.repeat(jnp.exp(draws), extent[dim] // blocks).reshape((-1,) + (1,) * (len(extent) - 1 - dim))
    return factor_of


def centred(stream_key, extent, spread, bound, cuts=(), kind=jnp.bfloat16):
    result = spread * jax.random.normal(stream_key, extent, jnp.float32)
    if cuts:
        result = result * shard_levels(stream_key, extent, cuts, -0.22, 0.18)
    return jnp.clip(result, -bound, bound).astype(kind)


def setup_inputs(seed: int = 0) -> dict:
    splits = jax.random.split(jax.random.key(seed), 8)
    tokens = centred(splits[0], (TOKENS, D), 1.0, 6.0, ((0, 256),))
    expert_ids = draw_expert_ids(jax.random.fold_in(splits[7], 71), 0)
    route_num = touch_ends(jax.random.randint(splits[2], (TOKENS, TOP), 1, DENOM + 1), jax.random.fold_in(splits[2], 1), 1, DENOM).astype(jnp.int32)
    w_gate = centred(splits[3], (EXPERTS, D, FF), D ** -0.5, 0.1875, ((0, 32),))
    w_up = centred(splits[4], (EXPERTS, D, FF), D ** -0.5, 0.1875, ((0, 32),))
    w_down = centred(splits[5], (EXPERTS, FF, D), FF ** -0.5, 0.3125, ((0, 32),))
    cotangent = centred(splits[6], (TOKENS, D), 0.2, 1.1953125, ((0, 256),))
    return {"tokens": tokens, "expert_ids": expert_ids, "route_num": route_num, "w_gate": w_gate, "w_up": w_up, "w_down": w_down, "cotangent": cotangent}


def rounded(value):
    return lax.optimization_barrier(value.astype(jnp.bfloat16)).astype(jnp.float32)


def group_sum(parts):
    return jnp.sum(parts.astype(jnp.float32), axis=0).astype(jnp.bfloat16)


def reference(tokens, expert_ids, route_num, w_gate, w_up, w_down, cotangent):
    highest = lax.Precision.HIGHEST
    group_tok = TOK_DEV * RANKS
    group_picks = group_tok * TOP
    rows_max = RANKS * CAP
    all_picks = TOKENS * TOP
    group_count = TOKENS // group_tok
    flat_ids = expert_ids.reshape(all_picks)
    route_weight = route_num.astype(jnp.float32) / DENOM
    flat_weight = route_weight.reshape(all_picks)

    def expert_group(expert, group, gate_w, up_w, down_w):
        first = (group * group_picks).astype(jnp.int32)
        chosen = lax.dynamic_slice_in_dim(flat_ids, first, group_picks)
        marked = (chosen == expert).astype(jnp.int32)
        order = (jnp.cumsum(marked) - 1).astype(jnp.int32)
        target = jnp.where(marked == 1, order, rows_max).astype(jnp.int32)
        local_pick = jnp.full((rows_max + 1,), group_picks, jnp.int32)
        local_pick = local_pick.at[target].set(jnp.arange(group_picks, dtype=jnp.int32))[:rows_max]
        filled = local_pick < group_picks
        pick_at = jnp.where(filled, first + local_pick, all_picks).astype(jnp.int32)
        safe_pick = jnp.minimum(pick_at, all_picks - 1).astype(jnp.int32)
        token_at = (safe_pick // TOP).astype(jnp.int32)
        weight_at = jnp.where(filled, flat_weight[safe_pick], jnp.float32(0.0))
        x_rows = jnp.where(filled[:, None], tokens[token_at].astype(jnp.float32), jnp.float32(0.0))
        grad_rows = rounded(weight_at[:, None] * cotangent[token_at].astype(jnp.float32))
        pre_gate = jnp.dot(x_rows, gate_w, precision=highest)
        pre_up = jnp.dot(x_rows, up_w, precision=highest)
        sigmoid_gate = jax.nn.sigmoid(pre_gate)
        activation = pre_gate * sigmoid_gate
        hidden = rounded(activation * pre_up)
        out_rows = jnp.dot(hidden, down_w, precision=highest).astype(jnp.bfloat16)
        hidden_grad = jnp.dot(grad_rows, down_w.T, precision=highest)
        gate_grad = rounded(hidden_grad * pre_up * sigmoid_gate * (1.0 + pre_gate * (1.0 - sigmoid_gate)))
        up_grad = rounded(hidden_grad * activation)
        pick_grad = (jnp.dot(gate_grad, gate_w.T, precision=highest) + jnp.dot(up_grad, up_w.T, precision=highest)).astype(jnp.bfloat16)
        gate_part = jnp.dot(x_rows.T, gate_grad, precision=highest).astype(jnp.bfloat16)
        up_part = jnp.dot(x_rows.T, up_grad, precision=highest).astype(jnp.bfloat16)
        down_part = jnp.dot(hidden.T, grad_rows, precision=highest).astype(jnp.bfloat16)
        return out_rows, pick_grad, pick_at, gate_part, up_part, down_part

    def expert_step(carry, expert):
        out_all, grad_all = carry
        gate_w = w_gate[expert].astype(jnp.float32)
        up_w = w_up[expert].astype(jnp.float32)
        down_w = w_down[expert].astype(jnp.float32)

        def one_group(group):
            return expert_group(expert, group, gate_w, up_w, down_w)

        out_rows, pick_grad, pick_at, gate_part, up_part, down_part = lax.map(one_group, jnp.arange(group_count, dtype=jnp.int32))
        flat_at = pick_at.reshape(-1)
        out_all = out_all.at[flat_at].set(out_rows.reshape(-1, D))
        grad_all = grad_all.at[flat_at].set(pick_grad.reshape(-1, D))
        return (out_all, grad_all), (group_sum(gate_part), group_sum(up_part), group_sum(down_part))

    start_rows = jnp.zeros((all_picks + 1, D), jnp.bfloat16)
    (out_all, grad_all), (gate_total, up_total, down_total) = lax.scan(expert_step, (start_rows, start_rows), jnp.arange(EXPERTS, dtype=jnp.int32))
    out_picks = out_all[:all_picks].reshape(TOKENS, TOP, D)
    grad_picks = grad_all[:all_picks].reshape(TOKENS, TOP, D)
    out_sum = jnp.zeros((TOKENS, D), jnp.float32)
    grad_sum = jnp.zeros((TOKENS, D), jnp.float32)
    for slot_k in range(TOP):
        out_sum = out_sum + route_weight[:, slot_k, None] * out_picks[:, slot_k].astype(jnp.float32)
        grad_sum = grad_sum + grad_picks[:, slot_k].astype(jnp.float32)
    return (out_sum.astype(jnp.bfloat16), grad_sum.astype(jnp.bfloat16), gate_total, up_total, down_total)
```

```python
import jax
import jax.numpy as jnp
from jax import lax
from jax.experimental import pallas as pl
from jax.experimental.pallas import tpu as pltpu
from jax.sharding import Mesh
from jax.sharding import PartitionSpec as P

DENOM = 256
Y, C, X, Z = 4, 2, 4, 8
AXES = ("y", "c", "x", "z")
TOK, D, FF, TOP, EXPERTS = 128, 1024, 384, 8, 32
SLOTS = 40
PAIR = 2 * SLOTS
ROWS = Z * PAIR
TILE = 128
SLICE = 9 * TILE
HALF = SLICE // 2
F32, BF16 = jnp.float32, jnp.bfloat16
VMEM_LIMIT = 60 * 1024 * 1024


def dot(a, b, dims):
    return lax.dot_general(a, b, (dims, ((), ())), preferred_element_type=F32)


NN = ((1,), (0,))
NT = ((1,), (1,))
TN = ((0,), (0,))


def move(value, target):
    pairs = []
    for y in range(Y):
        for c in range(C):
            for x in range(X):
                for z in range(Z):
                    to = target(y, c, x, z)
                    if to is None:
                        continue
                    ty, tc, tx, tz = to
                    src = ((y * C + c) * X + x) * Z + z
                    dst = (((ty % Y) * C + tc) * X + tx % X) * Z + tz % Z
                    pairs.append((src, dst))
    return lax.ppermute(value, AXES, pairs)


def z_right(v):
    return move(v, lambda y, c, x, z: (y, c, x, z + 1))


def z_left(v):
    return move(v, lambda y, c, x, z: (y, c, x, z - 1))


def y_right(v):
    return move(v, lambda y, c, x, z: (y + 1, c, x, z))


def y_left(v):
    return move(v, lambda y, c, x, z: (y - 1, c, x, z))


def swap(v):
    return move(v, lambda y, c, x, z: (y, 1 - c, x, z))


def call(body, out_shape, scratch, flops, nbytes, n_in, name, smem=0):
    vm = pl.BlockSpec(memory_space=pltpu.VMEM)
    sm = pl.BlockSpec(memory_space=pltpu.SMEM)
    return pl.pallas_call(
        body,
        out_shape=out_shape,
        in_specs=[sm] * smem + [vm] * n_in,
        out_specs=jax.tree.map(lambda _: vm, out_shape),
        scratch_shapes=scratch,
        compiler_params=pltpu.CompilerParams(vmem_limit_bytes=VMEM_LIMIT),
        cost_estimate=pl.CostEstimate(flops=flops, bytes_accessed=nbytes, transcendentals=0),
        name=name,
    )


def route_body(ids_ref, num_ref, out_ref):
    lanes = lax.broadcasted_iota(jnp.int32, (TOK, TILE), 1)
    total = jnp.zeros((TOK, TILE), F32)
    for k in range(TOP):
        weight = num_ref[:, k : k + 1].astype(F32) / DENOM
        total = total + jnp.where(lanes == ids_ref[:, k : k + 1], weight, 0.0)
    eye = (lanes == lax.broadcasted_iota(jnp.int32, (TOK, TILE), 0)).astype(BF16)
    out_ref[...] = dot(total.astype(BF16), eye, TN)[:EXPERTS].astype(BF16)


def plan_body(at_ref, routes_ref, target_ref, weight_ref):
    core, pos_x, pos_z = at_ref[0], at_ref[1], at_ref[2]
    before = (
        lax.broadcasted_iota(jnp.int32, (TOK, TOK), 0) < lax.broadcasted_iota(jnp.int32, (TOK, TOK), 1)
    ).astype(BF16)
    rows = lax.broadcasted_iota(jnp.int32, (EXPERTS, TOK), 0)
    for d in range(Z):
        for g in range(2):
            block = lax.rem(core + g, 2) * Z + lax.rem(pos_z + d, Z)
            routes = routes_ref[block].astype(F32)
            marked = routes > 0.0
            rank = dot(marked.astype(BF16), before, NN)
            rank = jnp.where(marked, rank + g * SLOTS, -1024.0)
            for s in range(2):
                expert = lax.rem(pos_x + 2 * core + s, X) * Z + pos_z
                mine = rows == expert
                row = jnp.sum(jnp.where(mine, rank, 0.0), axis=0, keepdims=True)
                wt = jnp.sum(jnp.where(mine, routes, 0.0), axis=0, keepdims=True)
                at = (d * 2 + s, slice(g * TOK, (g + 1) * TOK))
                target_ref[at[0] : at[0] + 1, at[1]] = row.astype(jnp.int32) + s * PAIR
                weight_ref[at[0] : at[0] + 1, at[1]] = wt


def one_hot(target_ref, weight_ref, d, weighted):
    slot = lax.broadcasted_iota(jnp.int32, (2 * PAIR, 2 * TOK), 0)
    first = slot == target_ref[2 * d : 2 * d + 1, :]
    second = slot == target_ref[2 * d + 1 : 2 * d + 2, :]
    if weighted:
        w0 = jnp.broadcast_to(weight_ref[2 * d : 2 * d + 1, :], slot.shape)
        w1 = jnp.broadcast_to(weight_ref[2 * d + 1 : 2 * d + 2, :], slot.shape)
        return jnp.where(first, w0, jnp.where(second, w1, 0.0)).astype(BF16)
    return (first | second).astype(F32).astype(BF16)


def collect(refs, target_ref, weight_ref, rows_ref, weighted):
    for d in range(Z):
        pick = one_hot(target_ref, weight_ref, d, weighted)
        both = jnp.concatenate([refs[d][...], refs[Z + d][...]], axis=0)
        got = dot(pick, both, NN).astype(BF16)
        rows_ref[0, d * PAIR : (d + 1) * PAIR, :] = got[:PAIR]
        rows_ref[1, d * PAIR : (d + 1) * PAIR, :] = got[PAIR:]


def spread(rows_ref, target_ref, weight_ref, own_ref, oth_ref, weighted):
    for d in range(Z):
        pick = one_hot(target_ref, weight_ref, d, weighted)
        both = jnp.concatenate(
            [rows_ref[0, d * PAIR : (d + 1) * PAIR, :], rows_ref[1, d * PAIR : (d + 1) * PAIR, :]], axis=0
        )
        total = dot(pick, both, TN).astype(BF16)
        own_ref[d] = total[:TOK]
        oth_ref[d] = total[TOK:]


CHUNK = 320


def forward_body(*refs):
    target_ref, weight_ref = refs[0], refs[1]
    tokens = refs[2 : 2 + 2 * Z]
    g0, g1, u0, u1, d0, d1 = refs[2 + 2 * Z : 8 + 2 * Z]
    own_ref, oth_ref, x_ref, pg_ref, pu_ref, h_ref, rows_ref = refs[8 + 2 * Z :]
    collect(tokens, target_ref, weight_ref, x_ref, False)
    for s, (g, u, dn) in enumerate(((g0, u0, d0), (g1, u1, d1))):

        @pl.loop(0, ROWS // CHUNK)
        def _(m):
            at = pl.ds(pl.multiple_of(m * CHUNK, CHUNK), CHUNK)
            rows = x_ref[s, at, :]
            pre_gate = dot(rows, g[0], NN)
            pre_up = dot(rows, u[0], NN)
            hidden = (pre_gate * jax.nn.sigmoid(pre_gate) * pre_up).astype(BF16)
            pg_ref[s, at, :] = pre_gate
            pu_ref[s, at, :] = pre_up
            h_ref[s, at, :] = hidden
            rows_ref[s, at, :] = dot(hidden, dn[0], NN).astype(BF16)

    spread(rows_ref, target_ref, weight_ref, own_ref, oth_ref, True)


def backward_body(*refs):
    target_ref, weight_ref = refs[0], refs[1]
    cots = refs[2 : 2 + 2 * Z]
    g0, g1, u0, u1, d0, d1, pg_ref, pu_ref = refs[2 + 2 * Z : 10 + 2 * Z]
    own_ref, oth_ref, c_ref, gg_ref, ug_ref, rows_ref = refs[10 + 2 * Z :]
    collect(cots, target_ref, weight_ref, c_ref, True)
    for s, (g, u, dn) in enumerate(((g0, u0, d0), (g1, u1, d1))):

        @pl.loop(0, ROWS // CHUNK)
        def _(m):
            at = pl.ds(pl.multiple_of(m * CHUNK, CHUNK), CHUNK)
            hidden_grad = dot(c_ref[s, at, :], dn[0], NT)
            pre_gate = pg_ref[s, at, :]
            pre_up = pu_ref[s, at, :]
            sg = jax.nn.sigmoid(pre_gate)
            gate_grad = (hidden_grad * pre_up * sg * (1.0 + pre_gate * (1.0 - sg))).astype(BF16)
            up_grad = (hidden_grad * (pre_gate * sg)).astype(BF16)
            gg_ref[s, at, :] = gate_grad
            ug_ref[s, at, :] = up_grad
            rows_ref[s, at, :] = (dot(gate_grad, g[0], NT) + dot(up_grad, u[0], NT)).astype(BF16)

    spread(rows_ref, target_ref, weight_ref, own_ref, oth_ref, False)


def weights_body(at_ref, x_ref, c_ref, h_ref, gg_ref, ug_ref, a_ref, b_ref):
    pos_y = at_ref[3]

    def put(s, part, first, value):
        rel = lax.rem(part // 2 + Y - pos_y, Y)
        for k in range(3):
            row = first + k * TILE
            tile = value[k].astype(BF16)
            low = max(0, min(TILE, HALF - row))
            if low > 0:
                a_ref[s, rel, part % 2, row : row + low, :] = tile[:low]
            if low < TILE:
                b_ref[rel, s, part % 2, row + low - HALF : row + TILE - HALF, :] = tile[low:]

    for s in range(2):
        for q in range(Y):
            cols = slice(q * 2 * TILE, (q + 1) * 2 * TILE)
            rows = x_ref[s, :, cols]
            gate = dot(rows, gg_ref[s], TN)
            up = dot(rows, ug_ref[s], TN)
            down = dot(h_ref[s], c_ref[s, :, cols], TN)
            for c in range(2):
                part = 2 * q + c
                lo = c * TILE
                put(s, part, 0, [gate[lo : lo + TILE, k * TILE : (k + 1) * TILE] for k in range(3)])
                put(s, part, 3 * TILE, [up[lo : lo + TILE, k * TILE : (k + 1) * TILE] for k in range(3)])
                put(s, part, 6 * TILE, [down[k * TILE : (k + 1) * TILE, lo : lo + TILE] for k in range(3)])


def add(*values):
    total = values[0].astype(F32)
    for value in values[1:]:
        total = total + value.astype(F32)
    return total.astype(BF16)


def gather_z(block):
    right, left = [block], [block]
    for _ in range(3):
        right.append(z_right(right[-1]))
        left.append(z_left(left[-1]))
    half = TOK // 2
    far = jnp.concatenate([z_right(right[3][:half]), z_left(left[3][half:])], axis=0)
    own = [block, left[1], left[2], left[3], far, right[3], right[2], right[1]]
    return own + [swap(v) for v in own]


def scatter_z(own, oth):
    got = swap(oth)
    half = TOK // 2
    far = add(own[4], got[4])
    from_left = z_right(far[:half])
    from_right = z_left(far[half:])
    part_r = add(own[3], got[3])
    part_r = jnp.concatenate([add(part_r[:half], from_left), part_r[half:]], axis=0)
    part_l = add(own[5], got[5])
    part_l = jnp.concatenate([part_l[:half], add(part_l[half:], from_right)], axis=0)
    from_left, from_right = z_right(part_r), z_left(part_l)
    for k in (2, 1):
        from_left, from_right = (
            z_right(add(own[k], got[k], from_left)),
            z_left(add(own[Z - k], got[Z - k], from_right)),
        )
    return add(own[0], got[0], from_left, from_right)


def x_up(v):
    return move(v, lambda y, c, x, z: (y, 0, x + 1, z) if c == 1 else None)


def x_down(v):
    return move(v, lambda y, c, x, z: (y, 1, x - 1, z) if c == 1 else None)


def x_merge(v):
    return move(v, lambda y, c, x, z: (y, 0, x + 1, z) if c == 0 else (y, 1, x - 1, z))


def reduce_x(first, second, core):
    half = first.shape[0] // 2
    top, bottom = x_up(first[:half]), x_down(first[half:])
    merged = jnp.concatenate([add(second[:half], top), add(second[half:], bottom)], axis=0)
    got = x_merge(merged)
    return add(jnp.where(core == 0, first, jnp.zeros_like(first)), got)


def reduce_core(v, core):
    first, second = v[..., 0, :, :], v[..., 1, :, :]
    keep = jnp.where(core == 0, first, second)
    send = jnp.where(core == 0, second, first)
    return add(keep, swap(send))


def reduce_y(v):
    n = v.shape[1] // 2
    top, bottom = y_right(v[2, :n]), y_left(v[2, n:])
    right = jnp.concatenate([add(v[1, :n], top), v[1, n:]], axis=0)
    left = jnp.concatenate([v[3, :n], add(v[3, n:], bottom)], axis=0)
    return add(v[0], y_right(right), y_left(left))


def local(tokens, expert_ids, route_num, w_gate, w_up, w_down, cotangent):
    core = lax.axis_index("c")
    at = jnp.stack([core, lax.axis_index("x"), lax.axis_index("z"), lax.axis_index("y")]).astype(jnp.int32)
    shape = jax.ShapeDtypeStruct
    routes = call(route_body, shape((EXPERTS, TOK), BF16), [], 10**6, 10**5, 2, "route")(expert_ids, route_num)
    routes = lax.all_gather(routes, ("c", "z"), tiled=False)
    target, weight = call(
        plan_body,
        (shape((2 * Z, 2 * TOK), jnp.int32), shape((2 * Z, 2 * TOK), F32)),
        [],
        10**7,
        10**5,
        1,
        "plan",
        smem=1,
    )(at, routes)

    def spread_weight(w):
        near = move(w, lambda y, c, x, z: (y, c, x - 1, z) if c == 0 else (y, c, x + 1, z))
        half = w.shape[1] // 2
        top = move(near[:, :half], lambda y, c, x, z: (y, 1, x - 1, z) if c == 0 else None)
        bottom = move(near[:, half:], lambda y, c, x, z: (y, 1, x + 1, z) if c == 1 else None)
        far = jnp.concatenate([top, bottom], axis=1)
        return jnp.where(core == 0, w, far), near

    all_tokens = gather_z(tokens)
    all_cots = gather_z(cotangent)
    weights = [*spread_weight(w_gate), *spread_weight(w_up), *spread_weight(w_down)]
    blocks = shape((Z, TOK, D), BF16)
    rows_d = shape((2, ROWS, D), BF16)
    rows_f = shape((2, ROWS, FF), F32)
    rows_h = shape((2, ROWS, FF), BF16)
    keep = pltpu.VMEM((2, ROWS, D), BF16)
    mults = 2 * ROWS * D * FF * 2
    own, oth, x_rows, pre_gate, pre_up, hidden = call(
        forward_body, (blocks, blocks, rows_d, rows_f, rows_f, rows_h), [keep], 3 * mults, 20 * 10**6, 24, "forward"
    )(target, weight, *all_tokens, *weights)
    output = scatter_z(own, oth)
    own, oth, c_rows, gate_grad, up_grad = call(
        backward_body, (blocks, blocks, rows_d, rows_h, rows_h), [keep], 3 * mults, 20 * 10**6, 26, "backward"
    )(target, weight, *all_cots, *weights, pre_gate, pre_up)
    tokens_grad = scatter_z(own, oth)
    parts_a, parts_b = shape((2, Y, 2, HALF, TILE), BF16), shape((Y, 2, 2, HALF, TILE), BF16)
    part_a, part_b = call(weights_body, (parts_a, parts_b), [], 3 * mults, 15 * 10**6, 5, "weights", smem=1)(
        at, x_rows, c_rows, hidden, gate_grad, up_grad
    )
    sum_a = reduce_x(part_a[0], part_a[1], core)
    sum_a = reduce_core(sum_a, core)
    sum_a = reduce_y(sum_a.reshape(Y, 2, HALF // 2, TILE)).reshape(HALF, TILE)
    sum_b = reduce_y(part_b)
    sum_b = reduce_x(sum_b[0], sum_b[1], core)
    sum_b = reduce_core(sum_b, core)
    total = jnp.concatenate([sum_a, sum_b], axis=0).reshape(3, 3, TILE, TILE)
    wide = lambda v: jnp.concatenate([v[0], v[1], v[2]], axis=1)[None]
    return output, tokens_grad, wide(total[0]), wide(total[1]), total[2].reshape(1, FF, TILE)


def solution(mesh):
    grid = Mesh(mesh.devices.reshape(Y, C, X, Z), AXES)
    rows = P(AXES, None)
    expert = P(("x", "z"), None, None)
    in_specs = (rows, rows, rows, expert, expert, expert, rows)
    out_specs = (
        rows,
        rows,
        P(("x", "z"), ("y", "c"), None),
        P(("x", "z"), ("y", "c"), None),
        P(("x", "z"), None, ("y", "c")),
    )
    return jax.shard_map(local, mesh=grid, in_specs=in_specs, out_specs=out_specs, check_vma=False)
```

```python
import jax
import jax.numpy as jnp
from jax import lax
from jax.experimental import pallas as pl
from jax.experimental.pallas import tpu as pltpu
from jax.sharding import Mesh
from jax.sharding import PartitionSpec as P

DENOM = 256
Y, C, X, Z = 4, 2, 4, 8
AXES = ("y", "c", "x", "z")
TOK, D, FF, TOP, EXPERTS = 128, 1024, 384, 8, 32
SLOTS = 40
PAIR = 2 * SLOTS
ROWS = Z * PAIR
TILE = 128
SLICE = 9 * TILE
HALF = SLICE // 2
F32, BF16 = jnp.float32, jnp.bfloat16
MIB = 1024 * 1024
MARK = 16
BLOCK = 2 * TOK + MARK
MARK_AT, TOK_AT = TOK, TOK + MARK


def dot(a, b, dims):
    return lax.dot_general(a, b, (dims, ((), ())), preferred_element_type=F32)


NN = ((1,), (0,))
NT = ((1,), (1,))
TN = ((0,), (0,))


def move(value, target):
    pairs = []
    for y in range(Y):
        for c in range(C):
            for x in range(X):
                for z in range(Z):
                    to = target(y, c, x, z)
                    if to is None:
                        continue
                    ty, tc, tx, tz = to
                    src = ((y * C + c) * X + x) * Z + z
                    dst = (((ty % Y) * C + tc) * X + tx % X) * Z + tz % Z
                    pairs.append((src, dst))
    return lax.ppermute(value, AXES, pairs)


def z_right(v):
    return move(v, lambda y, c, x, z: (y, c, x, z + 1 - 2 * c))


def z_left(v):
    return move(v, lambda y, c, x, z: (y, c, x, z - 1 + 2 * c))


def y_right(v):
    return move(v, lambda y, c, x, z: (y + 1, c, x, z))


def y_left(v):
    return move(v, lambda y, c, x, z: (y - 1, c, x, z))


def swap(v):
    return move(v, lambda y, c, x, z: (y, 1 - c, x, z))


def call(body, out_shape, scratch, flops, nbytes, n_in, name, vmem, smem=0, n_hbm=0):
    vm = pl.BlockSpec(memory_space=pltpu.VMEM)
    hbm = pl.BlockSpec(memory_space=pltpu.HBM)
    sm = pl.BlockSpec(memory_space=pltpu.SMEM)
    return pl.pallas_call(
        body,
        out_shape=out_shape,
        in_specs=[sm] * smem + [hbm] * n_hbm + [vm] * n_in,
        out_specs=jax.tree.map(lambda _: vm, out_shape),
        scratch_shapes=scratch,
        compiler_params=pltpu.CompilerParams(vmem_limit_bytes=vmem * MIB),
        cost_estimate=pl.CostEstimate(flops=flops, bytes_accessed=nbytes, transcendentals=0),
        name=name,
    )


def pack_body(ids_in, num_in, tok_ref, cot_ref, out_ref, ids_ref, num_ref, sems):
    copies = [
        pltpu.make_async_copy(cot_ref, out_ref.at[:TOK], sems.at[0]),
        pltpu.make_async_copy(tok_ref, out_ref.at[TOK_AT:], sems.at[1]),
        pltpu.make_async_copy(ids_in, ids_ref, sems.at[2]),
        pltpu.make_async_copy(num_in, num_ref, sems.at[3]),
    ]
    for copy in copies:
        copy.start()
    copies[2].wait()
    copies[3].wait()
    expert = lax.broadcasted_iota(jnp.int32, (EXPERTS, TOK), 0)
    table = jnp.zeros((EXPERTS, TOK), F32)
    for k in range(TOP):
        weight = num_ref[k : k + 1, :].astype(F32) / DENOM
        table = table + jnp.where(expert == ids_ref[k : k + 1, :], weight, 0.0)
    table = table.astype(BF16)
    out_ref[MARK_AT:TOK_AT, :TILE] = table[:MARK]
    out_ref[MARK_AT:TOK_AT, TILE : 2 * TILE] = table[MARK:]
    out_ref[MARK_AT:TOK_AT, 2 * TILE :] = jnp.zeros((MARK, D - 2 * TILE), BF16)
    for copy in copies[:2]:
        copy.wait()


def plan(at_ref, marks, target_ref, weight_ref):
    core, pos_x, pos_z = at_ref[0], at_ref[1], at_ref[2]
    before = (
        lax.broadcasted_iota(jnp.int32, (TOK, TOK), 0) < lax.broadcasted_iota(jnp.int32, (TOK, TOK), 1)
    ).astype(BF16)
    rows = lax.broadcasted_iota(jnp.int32, (EXPERTS, TOK), 0)
    for d in range(Z):
        for g in range(2):
            table = marks[g * Z + d]
            routes = jnp.concatenate([table[:, :TILE], table[:, TILE:]], axis=0).astype(F32)
            marked = routes > 0.0
            rank = dot(marked.astype(BF16), before, NN)
            rank = jnp.where(marked, rank + g * SLOTS, -1024.0)
            for s in range(2):
                expert = lax.rem(pos_x + 2 * core + s, X) * Z + pos_z
                mine = rows == expert
                row = jnp.sum(jnp.where(mine, rank, 0.0), axis=0, keepdims=True)
                wt = jnp.sum(jnp.where(mine, routes, 0.0), axis=0, keepdims=True)
                line, cols = d * 2 + s, slice(g * TOK, (g + 1) * TOK)
                target_ref[line : line + 1, cols] = row.astype(jnp.int32) + s * PAIR
                weight_ref[line : line + 1, cols] = wt


def one_hot(target_ref, weight_ref, d, weighted):
    slot = lax.broadcasted_iota(jnp.int32, (2 * PAIR, 2 * TOK), 0)
    first = slot == target_ref[2 * d : 2 * d + 1, :]
    second = slot == target_ref[2 * d + 1 : 2 * d + 2, :]
    if weighted:
        w0 = jnp.broadcast_to(weight_ref[2 * d : 2 * d + 1, :], slot.shape)
        w1 = jnp.broadcast_to(weight_ref[2 * d + 1 : 2 * d + 2, :], slot.shape)
        return jnp.where(first, w0, jnp.where(second, w1, 0.0)).astype(BF16)
    return (first | second).astype(F32).astype(BF16)


def collect(values, target_ref, weight_ref, rows_ref, weighted):
    for d in range(Z):
        pick = one_hot(target_ref, weight_ref, d, weighted)
        both = jnp.concatenate([values[d], values[Z + d]], axis=0)
        got = dot(pick, both, NN).astype(BF16)
        rows_ref[0, d * PAIR : (d + 1) * PAIR, :] = got[:PAIR]
        rows_ref[1, d * PAIR : (d + 1) * PAIR, :] = got[PAIR:]


GROUPS = ((4,), (3, 5), (2, 6), (1, 7), (0,))


def spread(rows_ref, target_ref, weight_ref, own_ref, oth_refs, weighted):
    at = slice(0, TOK) if weighted else slice(TOK, 2 * TOK)
    for d in range(Z):
        pick = one_hot(target_ref, weight_ref, d, weighted)
        both = jnp.concatenate(
            [rows_ref[0, d * PAIR : (d + 1) * PAIR, :], rows_ref[1, d * PAIR : (d + 1) * PAIR, :]], axis=0
        )
        total = dot(pick, both, TN).astype(BF16)
        own_ref[d, at, :] = total[:TOK]
        for group, ref in zip(GROUPS, oth_refs):
            if d in group:
                ref[group.index(d), at, :] = total[TOK:]


N_BLOCKS = 2 * (Z - 1) + 4


def expert_body(*refs):
    at_ref, refs = refs[0], refs[1:]
    blocks, refs = list(refs[:N_BLOCKS]), refs[N_BLOCKS:]
    g0, g1, u0, u1, d0, d1 = refs[:6]
    own_ref, oth_refs, refs = refs[6], refs[7:12], refs[12:]
    x_ref, c_ref, h_ref, gg_ref, ug_ref = refs[:5]
    out_rows, grad_rows, target_ref, weight_ref = refs[5:]
    toks, cots, marks = [], [], []
    for g in range(2):
        mine = blocks[g * (Z + 1) : (g + 1) * (Z + 1)]
        for d in range(Z):
            if d == 4:
                far_t, far_c = mine[4], mine[Z]
                marks.append(far_t[:MARK, : 2 * TILE])
                toks.append(far_t[MARK:, :])
                cots.append(far_c[...])
            else:
                ref = mine[d]
                marks.append(ref[MARK_AT:TOK_AT, : 2 * TILE])
                toks.append(ref[TOK_AT:, :])
                cots.append(ref[:TOK, :])
    plan(at_ref, marks, target_ref, weight_ref)
    collect(toks, target_ref, weight_ref, x_ref, False)
    collect(cots, target_ref, weight_ref, c_ref, True)
    for s, (g, u, dn) in enumerate(((g0, u0, d0), (g1, u1, d1))):
        rows = x_ref[s]
        pre_gate = dot(rows, g[0], NN)
        pre_up = dot(rows, u[0], NN)
        sg = jax.nn.sigmoid(pre_gate)
        silu = pre_gate * sg
        hidden = (silu * pre_up).astype(BF16)
        h_ref[s] = hidden
        out_rows[s] = dot(hidden, dn[0], NN).astype(BF16)
        hidden_grad = dot(c_ref[s], dn[0], NT)
        gate_grad = (hidden_grad * pre_up * sg * (1.0 + pre_gate * (1.0 - sg))).astype(BF16)
        up_grad = (hidden_grad * silu).astype(BF16)
        gg_ref[s] = gate_grad
        ug_ref[s] = up_grad
        grad_rows[s] = (dot(gate_grad, g[0], NT) + dot(up_grad, u[0], NT)).astype(BF16)
    spread(out_rows, target_ref, weight_ref, own_ref, oth_refs, True)
    spread(grad_rows, target_ref, weight_ref, own_ref, oth_refs, False)


def weights_body(at_ref, x_ref, c_ref, h_ref, gg_ref, ug_ref, a_ref, b_ref):
    pos_y = at_ref[3]

    def put(s, part, first, value):
        rel = lax.rem(part // 2 + Y - pos_y, Y)
        for k in range(3):
            row = first + k * TILE
            tile = value[k].astype(BF16)
            low = max(0, min(TILE, HALF - row))
            if low > 0:
                a_ref[s, rel, part % 2, row : row + low, :] = tile[:low]
            if low < TILE:
                b_ref[rel, s, part % 2, row + low - HALF : row + TILE - HALF, :] = tile[low:]

    for s in range(2):
        for q in range(Y):
            cols = slice(q * 2 * TILE, (q + 1) * 2 * TILE)
            rows = x_ref[s, :, cols]
            gate = dot(rows, gg_ref[s], TN)
            up = dot(rows, ug_ref[s], TN)
            down = dot(h_ref[s], c_ref[s, :, cols], TN)
            for c in range(2):
                part = 2 * q + c
                lo = c * TILE
                put(s, part, 0, [gate[lo : lo + TILE, k * TILE : (k + 1) * TILE] for k in range(3)])
                put(s, part, 3 * TILE, [up[lo : lo + TILE, k * TILE : (k + 1) * TILE] for k in range(3)])
                put(s, part, 6 * TILE, [down[k * TILE : (k + 1) * TILE, lo : lo + TILE] for k in range(3)])


def add(*values):
    total = values[0].astype(F32)
    for value in values[1:]:
        total = total + value.astype(F32)
    return total.astype(BF16)


def tie(*values):
    return lax.optimization_barrier(values)


def tie(*values):
    return lax.optimization_barrier(values)


def gather(block, weights):
    def near(w):
        return move(w, lambda y, c, x, z: (y, c, x - 1, z) if c == 0 else (y, c, x + 1, z))

    def far_down(w):
        return move(w, lambda y, c, x, z: (y, 1, x - 1, z) if c == 0 else (y, 0, x, z))

    def far_up(w):
        return move(w, lambda y, c, x, z: (y, 1, x + 1, z) if c == 1 else (y, 0, x, z))

    gate, up, down = weights
    right, left, gate_n, up_n, oth0 = tie(z_right(block), z_left(block), near(gate), near(up), swap(block))
    own, oth = {0: block, 7: right, 1: left}, {0: oth0}
    right, left, oth[7], oth[1], gate_f, up_f = tie(
        z_right(right), z_left(left), swap(right), swap(left), far_down(gate_n), far_up(up_n)
    )
    own[6], own[2] = right, left
    right, left, oth[6], oth[2], down_n = tie(z_right(right), z_left(left), swap(right), swap(left), near(down))
    own[5], own[3] = right, left
    far_t, far_c, oth[5], oth[3], down_f = tie(
        z_right(right[TOK:]), z_left(left[:TOK]), swap(right), swap(left), far_down(down_n)
    )
    own[4], oth[4] = far_t, swap(far_t)
    blocks = [own[d] for d in range(Z)] + [far_c] + [oth[d] for d in range(Z)] + [swap(far_c)]
    core = lax.axis_index("c")
    full = []
    for w, n, f in ((gate, gate_n, gate_f), (up, up_n, up_f), (down, down_n, down_f)):
        full += [jnp.where(core == 0, w, f), n]
    return blocks, full


def padded(got, first):
    zero = jnp.zeros((TOK, D), BF16)
    return jnp.concatenate([got, zero] if first else [zero, got], axis=0)


def x_merge(v):
    return move(v, lambda y, c, x, z: (y, 0, x + 1, z) if c == 0 else (y, 1, x - 1, z))


def pick(v, core, axis):
    first, second = (lax.index_in_dim(v, i, axis, keepdims=False) for i in range(2))
    return jnp.where(core == 0, first, second), jnp.where(core == 0, second, first)


def x_cross(v):
    return move(v, lambda y, c, x, z: (y, 1, x + 1, z) if c == 0 else (y, 0, x - 1, z))


def first_half(v, core):
    first, second = v
    (got,) = yield lambda: (move(first, lambda y, c, x, z: (y, 0, x + 1, z) if c == 1 else (y, 1, x, z)),)
    second = add(second, jnp.where(core == 0, got, jnp.zeros_like(got)))
    mine, other = pick(second, core, 1)
    keep, _ = pick(first, core, 1)
    one, two, three = yield lambda: (
        x_merge(mine),
        x_cross(other),
        move(first[:, 1], lambda y, c, x, z: (y, 1 - c, x, z)),
    )
    v = add(jnp.where(core == 0, keep, three), one, two)
    one, two, three = yield lambda: (
        y_right(v[1]),
        move(v[2], lambda y, c, x, z: (y + 2, c, x, z)),
        y_left(v[3]),
    )
    return add(v[0], one, two, three)


def second_half(v, core):
    (got,) = yield lambda: (y_left(v[2]),)
    left = add(v[3], got)
    right, left = yield lambda: (y_right(v[1]), y_left(left))
    first, second = add(v[0], right, left)
    mine, other = pick(second, core, 0)
    keep, send = pick(first, core, 0)
    one, two, three, four = yield lambda: (
        x_merge(mine),
        x_cross(other),
        move(send, lambda y, c, x, z: (y, 1, x, z) if c == 0 else (y, 0, x + 2, z)),
        move(keep, lambda y, c, x, z: (y, 1, x + 2, z) if c == 1 else (y, 0, x, z)),
    )
    return add(one, two, three, four)


def local(tokens, expert_ids, route_num, w_gate, w_up, w_down, cotangent):
    core = lax.axis_index("c")
    at = jnp.stack([core, lax.axis_index("x"), lax.axis_index("z"), lax.axis_index("y")]).astype(jnp.int32)
    shape = jax.ShapeDtypeStruct
    table = [pltpu.VMEM((TOP, TOK), jnp.int32), pltpu.VMEM((TOP, TOK), jnp.int32), pltpu.SemaphoreType.DMA((4,))]
    block = call(pack_body, shape((BLOCK, D), BF16), table, 10**6, 2 * 10**6, 0, "pack", 4, n_hbm=4)(
        expert_ids.T, route_num.T, tokens, cotangent
    )
    blocks, weights = gather(block, [w_gate, w_up, w_down])
    rows_d = shape((2, ROWS, D), BF16)
    rows_h = shape((2, ROWS, FF), BF16)
    mults = 2 * ROWS * D * FF * 2
    own, *oth, x_rows, c_rows, hidden, gate_grad, up_grad = call(
        expert_body,
        (
            shape((Z, 2 * TOK, D), BF16),
            *[shape((len(group), 2 * TOK, D), BF16) for group in GROUPS],
            rows_d,
            rows_d,
            rows_h,
            rows_h,
            rows_h,
        ),
        [
            pltpu.VMEM((2, ROWS, D), BF16),
            pltpu.VMEM((2, ROWS, D), BF16),
            pltpu.VMEM((2 * Z, 2 * TOK), jnp.int32),
            pltpu.VMEM((2 * Z, 2 * TOK), F32),
        ],
        6 * mults,
        30 * 10**6,
        N_BLOCKS + 6,
        "experts",
        20,
        smem=1,
    )(at, *blocks, *weights)
    near = swap(oth[0])[0]
    right, left = z_right(add(own[4][:TOK], near[:TOK])), z_left(add(own[4][TOK:], near[TOK:]))
    near = swap(oth[1])
    parts_a, parts_b = shape((2, Y, 2, HALF, TILE), BF16), shape((Y, 2, 2, HALF, TILE), BF16)
    part_a, part_b = call(weights_body, (parts_a, parts_b), [], 3 * mults, 15 * 10**6, 5, "weights", 16, smem=1)(
        at, x_rows, c_rows, hidden, gate_grad, up_grad
    )
    right, left, near, part_a, part_b = tie(right, left, near, part_a, part_b)
    halves = [first_half(part_a, core), second_half(part_b, core)]
    ready = [next(half) for half in halves]
    right, left = padded(right, True), padded(left, False)
    sums = [None, None]
    for k in range(3):
        right, left = add(own[3 - k], near[0], right), add(own[5 + k], near[1], left)
        right, left = z_right(right), z_left(left)
        near = swap(oth[2 + k])
        sent = [go() for go in ready]
        right, left, near, *flat = tie(right, left, near, *sent[0], *sent[1])
        for i, got in enumerate((flat[: len(sent[0])], flat[len(sent[0]) :])):
            try:
                ready[i] = halves[i].send(tuple(got))
            except StopIteration as stop:
                sums[i] = stop.value
    last = [own[0], near[0], right, left]
    output, tokens_grad = add(*[v[:TOK] for v in last]), add(*[v[TOK:] for v in last])
    total = jnp.concatenate([v.reshape(HALF, TILE) for v in sums], axis=0).reshape(3, 3, TILE, TILE)
    wide = lambda v: jnp.concatenate([v[0], v[1], v[2]], axis=1)[None]
    return output, tokens_grad, wide(total[0]), wide(total[1]), total[2].reshape(1, FF, TILE)


def solution(mesh):
    grid = Mesh(mesh.devices.reshape(Y, C, X, Z), AXES)
    rows = P(AXES, None)
    expert = P(("x", "z"), None, None)
    in_specs = (rows, rows, rows, expert, expert, expert, rows)
    out_specs = (
        rows,
        rows,
        P(("x", "z"), ("y", "c"), None),
        P(("x", "z"), ("y", "c"), None),
        P(("x", "z"), None, ("y", "c")),
    )
    return jax.shard_map(local, mesh=grid, in_specs=in_specs, out_specs=out_specs, check_vma=False)
```

```python
import functools

import jax
import jax.numpy as jnp
from jax import lax
from jax.experimental import pallas as pl
from jax.experimental.pallas import tpu as pltpu
from jax.sharding import Mesh
from jax.sharding import PartitionSpec as P

DENOM = 256
Y, C, X, Z = 4, 2, 4, 8
AXES = ("y", "c", "x", "z")
TOK, D, FF, TOP, EXPERTS = 128, 1024, 384, 8, 32
SLOTS = 40
PAIR = 2 * SLOTS
ROWS = Z * PAIR
TILE = 128
SLICE = 9 * TILE
A_ROWS = 672
B_ROWS = SLICE - A_ROWS
F32, BF16 = jnp.float32, jnp.bfloat16
MIB = 1024 * 1024
MARK = 16
BLOCK = 2 * TOK + MARK
MARK_AT, TOK_AT = TOK, TOK + MARK


def dot(a, b, dims):
    return lax.dot_general(a, b, (dims, ((), ())), preferred_element_type=F32)


NN = ((1,), (0,))
NT = ((1,), (1,))
TN = ((0,), (0,))


def move(value, target):
    pairs = []
    for y in range(Y):
        for c in range(C):
            for x in range(X):
                for z in range(Z):
                    to = target(y, c, x, z)
                    if to is None:
                        continue
                    ty, tc, tx, tz = to
                    src = ((y * C + c) * X + x) * Z + z
                    dst = (((ty % Y) * C + tc) * X + tx % X) * Z + tz % Z
                    pairs.append((src, dst))
    return lax.ppermute(value, AXES, pairs)


def z_right(v):
    return move(v, lambda y, c, x, z: (y, c, x, z + 1 - 2 * c))


def z_left(v):
    return move(v, lambda y, c, x, z: (y, c, x, z - 1 + 2 * c))


def y_right(v):
    return move(v, lambda y, c, x, z: (y + 1, c, x, z))


def y_left(v):
    return move(v, lambda y, c, x, z: (y - 1, c, x, z))


def swap(v):
    return move(v, lambda y, c, x, z: (y, 1 - c, x, z))


def call(body, out_shape, scratch, flops, nbytes, n_in, name, vmem, smem=0, n_hbm=0):
    vm = pl.BlockSpec(memory_space=pltpu.VMEM)
    hbm = pl.BlockSpec(memory_space=pltpu.HBM)
    sm = pl.BlockSpec(memory_space=pltpu.SMEM)
    return pl.pallas_call(
        body,
        out_shape=out_shape,
        in_specs=[sm] * smem + [hbm] * n_hbm + [vm] * n_in,
        out_specs=jax.tree.map(lambda _: vm, out_shape),
        scratch_shapes=scratch,
        compiler_params=pltpu.CompilerParams(vmem_limit_bytes=vmem * MIB),
        cost_estimate=pl.CostEstimate(flops=flops, bytes_accessed=nbytes, transcendentals=0),
        name=name,
    )


def pack_body(ids_in, num_in, tok_ref, cot_ref, out_ref, ids_ref, num_ref, sems):
    copies = [
        pltpu.make_async_copy(cot_ref, out_ref.at[:TOK], sems.at[0]),
        pltpu.make_async_copy(tok_ref, out_ref.at[TOK_AT:], sems.at[1]),
        pltpu.make_async_copy(ids_in, ids_ref, sems.at[2]),
        pltpu.make_async_copy(num_in, num_ref, sems.at[3]),
    ]
    for copy in copies:
        copy.start()
    copies[2].wait()
    copies[3].wait()
    expert = lax.broadcasted_iota(jnp.int32, (EXPERTS, TOK), 0)
    table = jnp.zeros((EXPERTS, TOK), F32)
    for k in range(TOP):
        weight = num_ref[k : k + 1, :].astype(F32) / DENOM
        table = table + jnp.where(expert == ids_ref[k : k + 1, :], weight, 0.0)
    table = table.astype(BF16)
    out_ref[MARK_AT:TOK_AT, :TILE] = table[:MARK]
    out_ref[MARK_AT:TOK_AT, TILE : 2 * TILE] = table[MARK:]
    out_ref[MARK_AT:TOK_AT, 2 * TILE :] = jnp.zeros((MARK, D - 2 * TILE), BF16)
    for copy in copies[:2]:
        copy.wait()


def plan(at_ref, marks, target_ref, weight_ref):
    n = len(marks) // 2
    core, pos_x, pos_z = at_ref[0], at_ref[1], at_ref[2]
    before = (
        lax.broadcasted_iota(jnp.int32, (TOK, TOK), 0) < lax.broadcasted_iota(jnp.int32, (TOK, TOK), 1)
    ).astype(BF16)
    rows = lax.broadcasted_iota(jnp.int32, (EXPERTS, TOK), 0)
    for d in range(n):
        for g in range(2):
            table = marks[g * n + d]
            routes = jnp.concatenate([table[:, :TILE], table[:, TILE:]], axis=0).astype(F32)
            marked = routes > 0.0
            rank = dot(marked.astype(BF16), before, NN)
            rank = jnp.where(marked, rank + g * SLOTS, -1024.0)
            for s in range(2):
                expert = lax.rem(pos_x + 2 * core + s, X) * Z + pos_z
                mine = rows == expert
                row = jnp.sum(jnp.where(mine, rank, 0.0), axis=0, keepdims=True)
                wt = jnp.sum(jnp.where(mine, routes, 0.0), axis=0, keepdims=True)
                line, cols = d * 2 + s, slice(g * TOK, (g + 1) * TOK)
                target_ref[line : line + 1, cols] = row.astype(jnp.int32) + s * PAIR
                weight_ref[line : line + 1, cols] = wt


def one_hot(target_ref, weight_ref, d, weighted):
    slot = lax.broadcasted_iota(jnp.int32, (2 * PAIR, 2 * TOK), 0)
    first = slot == target_ref[2 * d : 2 * d + 1, :]
    second = slot == target_ref[2 * d + 1 : 2 * d + 2, :]
    if weighted:
        w0 = jnp.broadcast_to(weight_ref[2 * d : 2 * d + 1, :], slot.shape)
        w1 = jnp.broadcast_to(weight_ref[2 * d + 1 : 2 * d + 2, :], slot.shape)
        return jnp.where(first, w0, jnp.where(second, w1, 0.0)).astype(BF16)
    return (first | second).astype(F32).astype(BF16)


def collect(values, target_ref, weight_ref, rows_ref, weighted):
    n = len(values) // 2
    for d in range(n):
        hot = one_hot(target_ref, weight_ref, d, weighted)
        both = jnp.concatenate([values[d], values[n + d]], axis=0)
        got = dot(hot, both, NN).astype(BF16)
        rows_ref[0, d * PAIR : (d + 1) * PAIR, :] = got[:PAIR]
        rows_ref[1, d * PAIR : (d + 1) * PAIR, :] = got[PAIR:]


def spread(rows_ref, target_ref, weight_ref, own_ref, oth_refs, groups, weighted):
    at = slice(0, TOK) if weighted else slice(TOK, 2 * TOK)
    d = 0
    for group, ref in zip(groups, oth_refs):
        for i in range(group):
            hot = one_hot(target_ref, weight_ref, d, weighted)
            both = jnp.concatenate(
                [rows_ref[0, d * PAIR : (d + 1) * PAIR, :], rows_ref[1, d * PAIR : (d + 1) * PAIR, :]], axis=0
            )
            total = dot(hot, both, TN).astype(BF16)
            own_ref[d, at, :] = total[:TOK]
            ref[i, at, :] = total[TOK:]
            d += 1


def expert_body(groups, split, *refs):
    n = sum(groups)
    at_ref, refs = refs[0], list(refs[1:])
    toks, cots, marks = [], [], []
    for _ in range(2):
        for d in range(n):
            if split and d == 0:
                part_t, part_c = refs.pop(0), refs.pop(0)
                marks.append(part_t[:MARK, : 2 * TILE])
                toks.append(part_t[MARK:, :])
                cots.append(part_c[...])
            else:
                ref = refs.pop(0)
                marks.append(ref[MARK_AT:TOK_AT, : 2 * TILE])
                toks.append(ref[TOK_AT:, :])
                cots.append(ref[:TOK, :])
    g0, g1, u0, u1, d0, d1, own_ref = refs[:7]
    oth_refs, refs = refs[7 : 7 + len(groups)], refs[7 + len(groups) :]
    x_ref, c_ref, h_ref, gg_ref, ug_ref, out_rows, grad_rows, target_ref, weight_ref = refs
    plan(at_ref, marks, target_ref, weight_ref)
    collect(toks, target_ref, weight_ref, x_ref, False)
    collect(cots, target_ref, weight_ref, c_ref, True)
    for s, (g, u, dn) in enumerate(((g0, u0, d0), (g1, u1, d1))):
        rows = x_ref[s]
        pre_gate = dot(rows, g[0], NN)
        pre_up = dot(rows, u[0], NN)
        sg = jax.nn.sigmoid(pre_gate)
        silu = pre_gate * sg
        hidden = (silu * pre_up).astype(BF16)
        h_ref[s] = hidden
        out_rows[s] = dot(hidden, dn[0], NN).astype(BF16)
        hidden_grad = dot(c_ref[s], dn[0], NT)
        gate_grad = (hidden_grad * pre_up * sg * (1.0 + pre_gate * (1.0 - sg))).astype(BF16)
        up_grad = (hidden_grad * silu).astype(BF16)
        gg_ref[s] = gate_grad
        ug_ref[s] = up_grad
        grad_rows[s] = (dot(gate_grad, g[0], NT) + dot(up_grad, u[0], NT)).astype(BF16)
    spread(out_rows, target_ref, weight_ref, own_ref, oth_refs, groups, True)
    spread(grad_rows, target_ref, weight_ref, own_ref, oth_refs, groups, False)


def experts(at, blocks, weights, groups, split, name):
    n = sum(groups)
    shape = jax.ShapeDtypeStruct
    rows_d, rows_h = shape((2, n * PAIR, D), BF16), shape((2, n * PAIR, FF), BF16)
    mults = 2 * n * PAIR * D * FF * 2
    own, *rest = call(
        functools.partial(expert_body, groups, split),
        (
            shape((n, 2 * TOK, D), BF16),
            *[shape((group, 2 * TOK, D), BF16) for group in groups],
            rows_d,
            rows_d,
            rows_h,
            rows_h,
            rows_h,
        ),
        [
            pltpu.VMEM((2, n * PAIR, D), BF16),
            pltpu.VMEM((2, n * PAIR, D), BF16),
            pltpu.VMEM((2 * n, 2 * TOK), jnp.int32),
            pltpu.VMEM((2 * n, 2 * TOK), F32),
        ],
        6 * mults,
        4 * n * 10**6,
        len(blocks) + 6,
        name,
        20,
        smem=1,
    )(at, *blocks, *weights)
    return own, rest[: len(groups)], rest[len(groups) :]


def weights_body(at_ref, *refs):
    pos_y = at_ref[3]
    parts, (a_ref, b_ref) = (refs[:5], refs[5:10]), refs[10:]

    def put(s, part, first, value):
        rel = lax.rem(part // 2 + Y - pos_y, Y)
        for k in range(3):
            row = first + k * TILE
            tile = value[k].astype(BF16)
            low = max(0, min(TILE, A_ROWS - row))
            if low > 0:
                a_ref[s, rel, part % 2, row : row + low, :] = tile[:low]
            if low < TILE:
                b_ref[rel, s, part % 2, row + low - A_ROWS : row + TILE - A_ROWS, :] = tile[low:]

    for s in range(2):
        for q in range(Y):
            cols = slice(q * 2 * TILE, (q + 1) * 2 * TILE)
            gate, up, down = (
                sum(terms)
                for terms in zip(
                    *[
                        (
                            dot(x_ref[s, :, cols], gg_ref[s], TN),
                            dot(x_ref[s, :, cols], ug_ref[s], TN),
                            dot(h_ref[s], c_ref[s, :, cols], TN),
                        )
                        for x_ref, c_ref, h_ref, gg_ref, ug_ref in parts
                    ]
                )
            )
            for c in range(2):
                part = 2 * q + c
                lo = c * TILE
                put(s, part, 0, [gate[lo : lo + TILE, k * TILE : (k + 1) * TILE] for k in range(3)])
                put(s, part, 3 * TILE, [up[lo : lo + TILE, k * TILE : (k + 1) * TILE] for k in range(3)])
                put(s, part, 6 * TILE, [down[k * TILE : (k + 1) * TILE, lo : lo + TILE] for k in range(3)])


def add(*values):
    total = values[0].astype(F32)
    for value in values[1:]:
        total = total + value.astype(F32)
    return total.astype(BF16)


def tie(*values):
    return lax.optimization_barrier(values)


def tie(*values):
    return lax.optimization_barrier(values)


def gather(at, block, weights):
    def near(w):
        return move(w, lambda y, c, x, z: (y, c, x - 1, z) if c == 0 else (y, c, x + 1, z))

    def far_down(w):
        return move(w, lambda y, c, x, z: (y, 1, x - 1, z) if c == 0 else (y, 0, x, z))

    def far_up(w):
        return move(w, lambda y, c, x, z: (y, 1, x + 1, z) if c == 1 else (y, 0, x, z))

    gate, up, down = weights
    right, left, gate_n, up_n, oth0 = tie(z_right(block), z_left(block), near(gate), near(up), swap(block))
    own, oth = {0: block, 7: right, 1: left}, {0: oth0}
    right, left, gate_f, up_f, down_n = tie(
        z_right(right), z_left(left), far_down(gate_n), far_up(up_n), near(down)
    )
    own[6], own[2] = right, left
    right, left, down_f, oth[7], oth[1], oth[6], oth[2] = tie(
        z_right(right), z_left(left), far_down(down_n), *[swap(own[d]) for d in (7, 1, 6, 2)]
    )
    own[5], own[3] = right, left
    core = lax.axis_index("c")
    full = []
    for w, n, f in ((gate, gate_n, gate_f), (up, up_n, up_f), (down, down_n, down_f)):
        full += [jnp.where(core == 0, w, f), n]
    spots = [2, 6, 1, 7, 0]
    near_work = experts(at, [own[d] for d in spots] + [oth[d] for d in spots], full, (2, 2, 1), False, "near")
    near_own, near_oth, near_rows = near_work
    far_t, far_c, oth[5], oth[3], near_own = tie(
        z_right(right[TOK:]), z_left(left[:TOK]), swap(right), swap(left), near_own
    )
    near_work = near_own, near_oth, near_rows
    far_work = experts(
        at,
        [far_t, far_c, own[3], own[5], swap(far_t), swap(far_c), oth[3], oth[5]],
        full,
        (1, 2),
        True,
        "far",
    )
    return near_work, far_work


def padded(got, first):
    zero = jnp.zeros((TOK, D), BF16)
    return jnp.concatenate([got, zero] if first else [zero, got], axis=0)


def x_merge(v):
    return move(v, lambda y, c, x, z: (y, 0, x + 1, z) if c == 0 else (y, 1, x - 1, z))


def pick(v, core, axis):
    first, second = (lax.index_in_dim(v, i, axis, keepdims=False) for i in range(2))
    return jnp.where(core == 0, first, second), jnp.where(core == 0, second, first)


def x_cross(v):
    return move(v, lambda y, c, x, z: (y, 1, x + 1, z) if c == 0 else (y, 0, x - 1, z))


def first_half(v, core):
    first, second = v
    (got,) = yield [(x_one, first)]
    three = got[:, 1]
    second = add(second, jnp.where(core == 0, got, jnp.zeros_like(got)))
    mine, other = pick(second, core, 1)
    keep, _ = pick(first, core, 1)
    one, two = yield [(x_merge, mine), (x_cross, other)]
    v = add(jnp.where(core == 0, keep, three), one, two)
    one, two, three = yield [(y_right, v[1]), (y_two, v[2]), (y_left, v[3])]
    return add(v[0], one, two, three)


def second_half(v, core):
    got, right = yield [(y_left, v[2]), (y_right, v[1])]
    (left,) = yield [(y_left, add(v[3], got))]
    first, second = add(v[0], right, left)
    got, two = yield [(x_merge, second), (x_two, first)]
    zero = jnp.zeros_like(first)
    v = add(got, jnp.where(core == 0, first, zero), jnp.where(core == 0, two, zero))
    keep, send = pick(v, core, 0)
    (got,) = yield [(swap, send)]
    return add(keep, got)


def x_one(v):
    return move(v, lambda y, c, x, z: (y, 0, x + 1, z) if c == 1 else (y, 1, x, z))


def x_two(v):
    return move(v, lambda y, c, x, z: (y, 0, x + 2, z) if c == 1 else (y, 1, x, z))


def y_two(v):
    return move(v, lambda y, c, x, z: (y + 2, c, x, z))


def local(tokens, expert_ids, route_num, w_gate, w_up, w_down, cotangent):
    core = lax.axis_index("c")
    at = jnp.stack([core, lax.axis_index("x"), lax.axis_index("z"), lax.axis_index("y")]).astype(jnp.int32)
    shape = jax.ShapeDtypeStruct
    table = [pltpu.VMEM((TOP, TOK), jnp.int32), pltpu.VMEM((TOP, TOK), jnp.int32), pltpu.SemaphoreType.DMA((4,))]
    block = call(pack_body, shape((BLOCK, D), BF16), table, 10**6, 2 * 10**6, 0, "pack", 4, n_hbm=4)(
        expert_ids.T, route_num.T, tokens, cotangent
    )
    near_work, far_work = gather(at, block, [w_gate, w_up, w_down])
    mults = 2 * ROWS * D * FF * 2
    own = dict(zip((4, 3, 5), far_work[0])) | dict(zip((2, 6, 1, 7, 0), near_work[0]))
    oth = far_work[1] + near_work[1]
    far_rows = list(far_work[2])
    near, far_rows[0] = tie(swap(oth[0]), far_rows[0])
    near = near[0]
    right, left = z_right(add(own[4][:TOK], near[:TOK])), z_left(add(own[4][TOK:], near[TOK:]))
    others = [swap(v) for v in oth[1:]]
    parts_a, parts_b = shape((2, Y, 2, A_ROWS, TILE), BF16), shape((Y, 2, 2, B_ROWS, TILE), BF16)
    part_a, part_b = call(weights_body, (parts_a, parts_b), [], 3 * mults, 15 * 10**6, 10, "weights", 16, smem=1)(
        at, *near_work[2], *far_rows
    )
    right, left, part_b, *others = tie(right, left, part_b, *others)

    def finish(work):
        step = next(work)
        while True:
            try:
                step = work.send(tuple(fn(value) for fn, value in step))
            except StopIteration as stop:
                return stop.value

    sum_a, sum_b = finish(first_half(part_a, core)), finish(second_half(part_b, core))
    right, left = padded(right, True), padded(left, False)
    for k in (3, 2, 1):
        near = others.pop(0)
        right, left = add(own[k], near[0], right), add(own[Z - k], near[1], left)
        right, left = tie(z_right(right), z_left(left))
    last = [own[0], others[0][0], right, left]
    output, tokens_grad = add(*[v[:TOK] for v in last]), add(*[v[TOK:] for v in last])
    total = jnp.concatenate([sum_a.reshape(A_ROWS, TILE), sum_b.reshape(B_ROWS, TILE)], axis=0).reshape(3, 3, TILE, TILE)
    wide = lambda v: jnp.concatenate([v[0], v[1], v[2]], axis=1)[None]
    return output, tokens_grad, wide(total[0]), wide(total[1]), total[2].reshape(1, FF, TILE)


def solution(mesh):
    grid = Mesh(mesh.devices.reshape(Y, C, X, Z), AXES)
    rows = P(AXES, None)
    expert = P(("x", "z"), None, None)
    in_specs = (rows, rows, rows, expert, expert, expert, rows)
    out_specs = (
        rows,
        rows,
        P(("x", "z"), ("y", "c"), None),
        P(("x", "z"), ("y", "c"), None),
        P(("x", "z"), None, ("y", "c")),
    )
    return jax.shard_map(local, mesh=grid, in_specs=in_specs, out_specs=out_specs, check_vma=False)
```

```python
import functools

import jax
import jax.numpy as jnp
from jax import lax
from jax.experimental import pallas as pl
from jax.experimental.pallas import tpu as pltpu
from jax.sharding import Mesh
from jax.sharding import PartitionSpec as P

DENOM = 256
Y, C, X, Z = 4, 2, 4, 8
AXES = ("y", "c", "x", "z")
TOK, D, FF, TOP, EXPERTS = 128, 1024, 384, 8, 32
SLOTS = 40
PAIR = 2 * SLOTS
ROWS = Z * PAIR
TILE = 128
SLICE = 9 * TILE
A_ROWS = 672
B_ROWS = SLICE - A_ROWS
F32, BF16 = jnp.float32, jnp.bfloat16
MIB = 1024 * 1024
MARK = 16
BLOCK = 2 * TOK + MARK
MARK_AT, TOK_AT = TOK, TOK + MARK


def dot(a, b, dims):
    return lax.dot_general(a, b, (dims, ((), ())), preferred_element_type=F32)


NN = ((1,), (0,))
NT = ((1,), (1,))
TN = ((0,), (0,))


def move(value, target):
    pairs = []
    for y in range(Y):
        for c in range(C):
            for x in range(X):
                for z in range(Z):
                    to = target(y, c, x, z)
                    if to is None:
                        continue
                    ty, tc, tx, tz = to
                    src = ((y * C + c) * X + x) * Z + z
                    dst = (((ty % Y) * C + tc) * X + tx % X) * Z + tz % Z
                    pairs.append((src, dst))
    return lax.ppermute(value, AXES, pairs)


def z_right(v):
    return move(v, lambda y, c, x, z: (y, c, x, z + 1 - 2 * c))


def z_left(v):
    return move(v, lambda y, c, x, z: (y, c, x, z - 1 + 2 * c))


def y_right(v):
    return move(v, lambda y, c, x, z: (y + 1, c, x, z))


def y_left(v):
    return move(v, lambda y, c, x, z: (y - 1, c, x, z))


def swap(v):
    return move(v, lambda y, c, x, z: (y, 1 - c, x, z))


def call(body, out_shape, scratch, flops, nbytes, n_in, name, vmem, smem=0, n_hbm=0):
    vm = pl.BlockSpec(memory_space=pltpu.VMEM)
    hbm = pl.BlockSpec(memory_space=pltpu.HBM)
    sm = pl.BlockSpec(memory_space=pltpu.SMEM)
    return pl.pallas_call(
        body,
        out_shape=out_shape,
        in_specs=[sm] * smem + [hbm] * n_hbm + [vm] * n_in,
        out_specs=jax.tree.map(lambda _: vm, out_shape),
        scratch_shapes=scratch,
        compiler_params=pltpu.CompilerParams(vmem_limit_bytes=vmem * MIB),
        cost_estimate=pl.CostEstimate(flops=flops, bytes_accessed=nbytes, transcendentals=0),
        name=name,
    )


def pack_body(ids_in, num_in, tok_ref, cot_ref, out_ref, ids_ref, num_ref, sems):
    copies = [
        pltpu.make_async_copy(cot_ref, out_ref.at[:TOK], sems.at[0]),
        pltpu.make_async_copy(tok_ref, out_ref.at[TOK_AT:], sems.at[1]),
        pltpu.make_async_copy(ids_in, ids_ref, sems.at[2]),
        pltpu.make_async_copy(num_in, num_ref, sems.at[3]),
    ]
    for copy in copies:
        copy.start()
    copies[2].wait()
    copies[3].wait()
    expert = lax.broadcasted_iota(jnp.int32, (EXPERTS, TOK), 0)
    table = jnp.zeros((EXPERTS, TOK), F32)
    for k in range(TOP):
        weight = num_ref[k : k + 1, :].astype(F32) / DENOM
        table = table + jnp.where(expert == ids_ref[k : k + 1, :], weight, 0.0)
    table = table.astype(BF16)
    out_ref[MARK_AT:TOK_AT, :TILE] = table[:MARK]
    out_ref[MARK_AT:TOK_AT, TILE : 2 * TILE] = table[MARK:]
    out_ref[MARK_AT:TOK_AT, 2 * TILE :] = jnp.zeros((MARK, D - 2 * TILE), BF16)
    for copy in copies[:2]:
        copy.wait()


def plan(at_ref, marks, target_ref, weight_ref):
    n = len(marks) // 2
    core, pos_x, pos_z = at_ref[0], at_ref[1], at_ref[2]
    before = (
        lax.broadcasted_iota(jnp.int32, (TOK, TOK), 0) < lax.broadcasted_iota(jnp.int32, (TOK, TOK), 1)
    ).astype(BF16)
    rows = lax.broadcasted_iota(jnp.int32, (EXPERTS, TOK), 0)
    for d in range(n):
        for g in range(2):
            table = marks[g * n + d]
            routes = jnp.concatenate([table[:, :TILE], table[:, TILE:]], axis=0).astype(F32)
            marked = routes > 0.0
            rank = dot(marked.astype(BF16), before, NN)
            rank = jnp.where(marked, rank + g * SLOTS, -1024.0)
            for s in range(2):
                expert = lax.rem(pos_x + 2 * core + s, X) * Z + pos_z
                mine = rows == expert
                row = jnp.sum(jnp.where(mine, rank, 0.0), axis=0, keepdims=True)
                wt = jnp.sum(jnp.where(mine, routes, 0.0), axis=0, keepdims=True)
                line, cols = d * 2 + s, slice(g * TOK, (g + 1) * TOK)
                target_ref[line : line + 1, cols] = row.astype(jnp.int32) + s * PAIR
                weight_ref[line : line + 1, cols] = wt


def one_hot(target_ref, weight_ref, d, weighted):
    slot = lax.broadcasted_iota(jnp.int32, (2 * PAIR, 2 * TOK), 0)
    first = slot == target_ref[2 * d : 2 * d + 1, :]
    second = slot == target_ref[2 * d + 1 : 2 * d + 2, :]
    if weighted:
        w0 = jnp.broadcast_to(weight_ref[2 * d : 2 * d + 1, :], slot.shape)
        w1 = jnp.broadcast_to(weight_ref[2 * d + 1 : 2 * d + 2, :], slot.shape)
        return jnp.where(first, w0, jnp.where(second, w1, 0.0)).astype(BF16)
    return (first | second).astype(F32).astype(BF16)


def collect(values, target_ref, weight_ref, rows_ref, weighted):
    n = len(values) // 2
    for d in range(n):
        hot = one_hot(target_ref, weight_ref, d, weighted)
        both = jnp.concatenate([values[d], values[n + d]], axis=0)
        got = dot(hot, both, NN).astype(BF16)
        rows_ref[0, d * PAIR : (d + 1) * PAIR, :] = got[:PAIR]
        rows_ref[1, d * PAIR : (d + 1) * PAIR, :] = got[PAIR:]


def spread(rows_ref, target_ref, weight_ref, own_ref, oth_refs, groups, weighted):
    at = slice(0, TOK) if weighted else slice(TOK, 2 * TOK)
    d = 0
    for group, ref in zip(groups, oth_refs):
        for i in range(group):
            hot = one_hot(target_ref, weight_ref, d, weighted)
            both = jnp.concatenate(
                [rows_ref[0, d * PAIR : (d + 1) * PAIR, :], rows_ref[1, d * PAIR : (d + 1) * PAIR, :]], axis=0
            )
            total = dot(hot, both, TN).astype(BF16)
            own_ref[d, at, :] = total[:TOK]
            ref[i, at, :] = total[TOK:]
            d += 1


def expert_body(groups, split, *refs):
    n = sum(groups)
    at_ref, refs = refs[0], list(refs[1:])
    toks, cots, marks = [], [], []
    for _ in range(2):
        for d in range(n):
            if split and d == 0:
                part_t, part_c = refs.pop(0), refs.pop(0)
                marks.append(part_t[:MARK, : 2 * TILE])
                toks.append(part_t[MARK:, :])
                cots.append(part_c[...])
            else:
                ref = refs.pop(0)
                marks.append(ref[MARK_AT:TOK_AT, : 2 * TILE])
                toks.append(ref[TOK_AT:, :])
                cots.append(ref[:TOK, :])
    w0, w1, d0, d1, own_ref = refs[:5]
    oth_refs, refs = refs[5 : 5 + len(groups)], refs[5 + len(groups) :]
    x_ref, c_ref, h_ref, gu_ref, out_rows, grad_rows, target_ref, weight_ref = refs
    plan(at_ref, marks, target_ref, weight_ref)
    collect(toks, target_ref, weight_ref, x_ref, False)
    collect(cots, target_ref, weight_ref, c_ref, True)
    for s, (w, dn) in enumerate(((w0, d0), (w1, d1))):
        rows = x_ref[s]
        both = dot(rows, w[0], NN)
        pre_gate, pre_up = both[:, :FF], both[:, FF:]
        sg = jax.nn.sigmoid(pre_gate)
        silu = pre_gate * sg
        hidden = (silu * pre_up).astype(BF16)
        h_ref[s] = hidden
        out_rows[s] = dot(hidden, dn[0], NN).astype(BF16)
        hidden_grad = dot(c_ref[s], dn[0], NT)
        gate_grad = (hidden_grad * pre_up * sg * (1.0 + pre_gate * (1.0 - sg))).astype(BF16)
        up_grad = (hidden_grad * silu).astype(BF16)
        gu_ref[s, :, :FF] = gate_grad
        gu_ref[s, :, FF:] = up_grad
        grad_rows[s] = dot(gu_ref[s], w[0], NT).astype(BF16)
    spread(out_rows, target_ref, weight_ref, own_ref, oth_refs, groups, True)
    spread(grad_rows, target_ref, weight_ref, own_ref, oth_refs, groups, False)


def experts(at, blocks, weights, groups, split, name):
    n = sum(groups)
    shape = jax.ShapeDtypeStruct
    rows_d, rows_h = shape((2, n * PAIR, D), BF16), shape((2, n * PAIR, FF), BF16)
    mults = 2 * n * PAIR * D * FF * 2
    own, *rest = call(
        functools.partial(expert_body, groups, split),
        (
            shape((n, 2 * TOK, D), BF16),
            *[shape((group, 2 * TOK, D), BF16) for group in groups],
            rows_d,
            rows_d,
            rows_h,
            shape((2, n * PAIR, 2 * FF), BF16),
        ),
        [
            pltpu.VMEM((2, n * PAIR, D), BF16),
            pltpu.VMEM((2, n * PAIR, D), BF16),
            pltpu.VMEM((2 * n, 2 * TOK), jnp.int32),
            pltpu.VMEM((2 * n, 2 * TOK), F32),
        ],
        6 * mults,
        4 * n * 10**6,
        len(blocks) + 4,
        name,
        20,
        smem=1,
    )(at, *blocks, *weights)
    return own, rest[: len(groups)], rest[len(groups) :]


def weights_body(at_ref, *refs):
    pos_y = at_ref[3]
    parts, (a_ref, b_ref) = (refs[:4], refs[4:8]), refs[8:]

    def put(s, part, first, value):
        rel = lax.rem(part // 2 + Y - pos_y, Y)
        for k in range(3):
            row = first + k * TILE
            tile = value[k].astype(BF16)
            low = max(0, min(TILE, A_ROWS - row))
            if low > 0:
                a_ref[s, rel, part % 2, row : row + low, :] = tile[:low]
            if low < TILE:
                b_ref[rel, s, part % 2, row + low - A_ROWS : row + TILE - A_ROWS, :] = tile[low:]

    for s in range(2):
        for q in range(Y):
            cols = slice(q * 2 * TILE, (q + 1) * 2 * TILE)
            both, down = (
                sum(terms)
                for terms in zip(
                    *[
                        (dot(x_ref[s, :, cols], gu_ref[s], TN), dot(h_ref[s], c_ref[s, :, cols], TN))
                        for x_ref, c_ref, h_ref, gu_ref in parts
                    ]
                )
            )
            gate, up = both[:, :FF], both[:, FF:]
            for c in range(2):
                part = 2 * q + c
                lo = c * TILE
                put(s, part, 0, [gate[lo : lo + TILE, k * TILE : (k + 1) * TILE] for k in range(3)])
                put(s, part, 3 * TILE, [up[lo : lo + TILE, k * TILE : (k + 1) * TILE] for k in range(3)])
                put(s, part, 6 * TILE, [down[k * TILE : (k + 1) * TILE, lo : lo + TILE] for k in range(3)])


def add(*values):
    total = values[0].astype(F32)
    for value in values[1:]:
        total = total + value.astype(F32)
    return total.astype(BF16)


def tie(*values):
    return lax.optimization_barrier(values)


def tie(*values):
    return lax.optimization_barrier(values)


def gather(at, block, weights):
    def near(w):
        return move(w, lambda y, c, x, z: (y, c, x - 1, z) if c == 0 else (y, c, x + 1, z))

    def far_down(w):
        return move(w, lambda y, c, x, z: (y, 1, x - 1, z) if c == 0 else (y, 0, x, z))

    def far_up(w):
        return move(w, lambda y, c, x, z: (y, 1, x + 1, z) if c == 1 else (y, 0, x, z))

    gate, up, down = weights
    right, left, gate_n, up_n, oth0 = tie(z_right(block), z_left(block), near(gate), near(up), swap(block))
    own, oth = {0: block, 7: right, 1: left}, {0: oth0}
    right, left, gate_f, up_f, down_n = tie(
        z_right(right), z_left(left), far_down(gate_n), far_up(up_n), near(down)
    )
    own[6], own[2] = right, left
    core = lax.axis_index("c")
    wide_s = jnp.where(core == 0, jnp.concatenate([gate, up], axis=2), jnp.concatenate([gate_f, up_f], axis=2))
    wide_n = jnp.concatenate([gate_n, up_n], axis=2)
    oth[6], oth[2] = swap(own[6]), swap(own[2])
    right, left, down_f, oth[7], oth[1], wide_s, wide_n = tie(
        z_right(right), z_left(left), far_down(down_n), swap(own[7]), swap(own[1]), wide_s, wide_n
    )
    own[5], own[3] = right, left
    full = [wide_s, wide_n, jnp.where(core == 0, down, down_f), down_n]
    spots = [2, 6, 1, 7, 0]
    near_work = experts(at, [own[d] for d in spots] + [oth[d] for d in spots], full, (2, 2, 1), False, "near")
    near_own, near_oth, near_rows = near_work
    far_t, far_c, oth[5], oth[3], near_own = tie(
        z_right(right[TOK:]), z_left(left[:TOK]), swap(right), swap(left), near_own
    )
    near_work = near_own, near_oth, near_rows
    far_work = experts(
        at,
        [far_t, far_c, own[3], own[5], swap(far_t), swap(far_c), oth[3], oth[5]],
        full,
        (1, 2),
        True,
        "far",
    )
    return near_work, far_work


def padded(got, first):
    zero = jnp.zeros((TOK, D), BF16)
    return jnp.concatenate([got, zero] if first else [zero, got], axis=0)


def x_merge(v):
    return move(v, lambda y, c, x, z: (y, 0, x + 1, z) if c == 0 else (y, 1, x - 1, z))


def pick(v, core, axis):
    first, second = (lax.index_in_dim(v, i, axis, keepdims=False) for i in range(2))
    return jnp.where(core == 0, first, second), jnp.where(core == 0, second, first)


def x_cross(v):
    return move(v, lambda y, c, x, z: (y, 1, x + 1, z) if c == 0 else (y, 0, x - 1, z))


def first_half(v, core):
    first, second = v
    (got,) = yield [(x_one, first)]
    three = got[:, 1]
    second = add(second, jnp.where(core == 0, got, jnp.zeros_like(got)))
    mine, other = pick(second, core, 1)
    keep, _ = pick(first, core, 1)
    one, two = yield [(x_merge, mine), (x_cross, other)]
    v = add(jnp.where(core == 0, keep, three), one, two)
    one, two, three = yield [(y_right, v[1]), (y_two, v[2]), (y_left, v[3])]
    return add(v[0], one, two, three)


def second_half(v, core):
    got, right = yield [(y_left, v[2]), (y_right, v[1])]
    (left,) = yield [(y_left, add(v[3], got))]
    first, second = add(v[0], right, left)
    got, two = yield [(x_merge, second), (x_two, first)]
    zero = jnp.zeros_like(first)
    v = add(got, jnp.where(core == 0, first, zero), jnp.where(core == 0, two, zero))
    keep, send = pick(v, core, 0)
    (got,) = yield [(swap, send)]
    return add(keep, got)


def x_one(v):
    return move(v, lambda y, c, x, z: (y, 0, x + 1, z) if c == 1 else (y, 1, x, z))


def x_two(v):
    return move(v, lambda y, c, x, z: (y, 0, x + 2, z) if c == 1 else (y, 1, x, z))


def y_two(v):
    return move(v, lambda y, c, x, z: (y + 2, c, x, z))


def local(tokens, expert_ids, route_num, w_gate, w_up, w_down, cotangent):
    core = lax.axis_index("c")
    at = jnp.stack([core, lax.axis_index("x"), lax.axis_index("z"), lax.axis_index("y")]).astype(jnp.int32)
    shape = jax.ShapeDtypeStruct
    table = [pltpu.VMEM((TOP, TOK), jnp.int32), pltpu.VMEM((TOP, TOK), jnp.int32), pltpu.SemaphoreType.DMA((4,))]
    block = call(pack_body, shape((BLOCK, D), BF16), table, 10**6, 2 * 10**6, 0, "pack", 4, n_hbm=4)(
        expert_ids.T, route_num.T, tokens, cotangent
    )
    near_work, far_work = gather(at, block, [w_gate, w_up, w_down])
    mults = 2 * ROWS * D * FF * 2
    own = dict(zip((4, 3, 5), far_work[0])) | dict(zip((2, 6, 1, 7, 0), near_work[0]))
    oth = far_work[1] + near_work[1]
    far_rows = list(far_work[2])
    near, far_rows[0] = tie(swap(oth[0]), far_rows[0])
    near = near[0]
    right, left = z_right(add(own[4][:TOK], near[:TOK])), z_left(add(own[4][TOK:], near[TOK:]))
    others = [swap(v) for v in oth[1:]]
    parts_a, parts_b = shape((2, Y, 2, A_ROWS, TILE), BF16), shape((Y, 2, 2, B_ROWS, TILE), BF16)
    part_a, part_b = call(weights_body, (parts_a, parts_b), [], 3 * mults, 15 * 10**6, 8, "weights", 16, smem=1)(
        at, *near_work[2], *far_rows
    )
    right, left, part_b, *others = tie(right, left, part_b, *others)

    def finish(work):
        step = next(work)
        while True:
            try:
                step = work.send(tuple(fn(value) for fn, value in step))
            except StopIteration as stop:
                return stop.value

    sum_a, sum_b = finish(first_half(part_a, core)), finish(second_half(part_b, core))
    right, left = padded(right, True), padded(left, False)
    for k in (3, 2, 1):
        near = others.pop(0)
        right, left = add(own[k], near[0], right), add(own[Z - k], near[1], left)
        right, left = tie(z_right(right), z_left(left))
    last = [own[0], others[0][0], right, left]
    output, tokens_grad = add(*[v[:TOK] for v in last]), add(*[v[TOK:] for v in last])
    total = jnp.concatenate([sum_a.reshape(A_ROWS, TILE), sum_b.reshape(B_ROWS, TILE)], axis=0).reshape(3, 3, TILE, TILE)
    wide = lambda v: jnp.concatenate([v[0], v[1], v[2]], axis=1)[None]
    return output, tokens_grad, wide(total[0]), wide(total[1]), total[2].reshape(1, FF, TILE)


def solution(mesh):
    grid = Mesh(mesh.devices.reshape(Y, C, X, Z), AXES)
    rows = P(AXES, None)
    expert = P(("x", "z"), None, None)
    in_specs = (rows, rows, rows, expert, expert, expert, rows)
    out_specs = (
        rows,
        rows,
        P(("x", "z"), ("y", "c"), None),
        P(("x", "z"), ("y", "c"), None),
        P(("x", "z"), None, ("y", "c")),
    )
    return jax.shard_map(local, mesh=grid, in_specs=in_specs, out_specs=out_specs, check_vma=False)
```

```python
import functools

import jax
import jax.numpy as jnp
from jax import lax
from jax.experimental import pallas as pl
from jax.experimental.pallas import tpu as pltpu
from jax.sharding import Mesh
from jax.sharding import PartitionSpec as P

DENOM = 256
Y, C, X, Z = 4, 2, 4, 8
AXES = ("y", "c", "x", "z")
TOK, D, FF, TOP, EXPERTS = 128, 1024, 384, 8, 32
SLOTS = 40
PAIR = 2 * SLOTS
ROWS = Z * PAIR
TILE = 128
SLICE = 9 * TILE
A_ROWS = 672
B_ROWS = SLICE - A_ROWS
F32, BF16 = jnp.float32, jnp.bfloat16
MIB = 1024 * 1024
MARK = 16
BLOCK = 2 * TOK + MARK
MARK_AT, TOK_AT = TOK, TOK + MARK


def dot(a, b, dims):
    return lax.dot_general(a, b, (dims, ((), ())), preferred_element_type=F32)


NN = ((1,), (0,))
NT = ((1,), (1,))
TN = ((0,), (0,))


def move(value, target):
    pairs = []
    for y in range(Y):
        for c in range(C):
            for x in range(X):
                for z in range(Z):
                    to = target(y, c, x, z)
                    if to is None:
                        continue
                    ty, tc, tx, tz = to
                    src = ((y * C + c) * X + x) * Z + z
                    dst = (((ty % Y) * C + tc) * X + tx % X) * Z + tz % Z
                    pairs.append((src, dst))
    return lax.ppermute(value, AXES, pairs)


def z_right(v):
    return move(v, lambda y, c, x, z: (y, c, x, z + 1 - 2 * c))


def z_left(v):
    return move(v, lambda y, c, x, z: (y, c, x, z - 1 + 2 * c))


def y_right(v):
    return move(v, lambda y, c, x, z: (y + 1, c, x, z))


def y_left(v):
    return move(v, lambda y, c, x, z: (y - 1, c, x, z))


def swap(v):
    return move(v, lambda y, c, x, z: (y, 1 - c, x, z))


def call(body, out_shape, scratch, flops, nbytes, n_in, name, vmem, smem=0, n_hbm=0):
    vm = pl.BlockSpec(memory_space=pltpu.VMEM)
    hbm = pl.BlockSpec(memory_space=pltpu.HBM)
    sm = pl.BlockSpec(memory_space=pltpu.SMEM)
    return pl.pallas_call(
        body,
        out_shape=out_shape,
        in_specs=[sm] * smem + [hbm] * n_hbm + [vm] * n_in,
        out_specs=jax.tree.map(lambda _: vm, out_shape),
        scratch_shapes=scratch,
        compiler_params=pltpu.CompilerParams(vmem_limit_bytes=vmem * MIB),
        cost_estimate=pl.CostEstimate(flops=flops, bytes_accessed=nbytes, transcendentals=0),
        name=name,
    )


def pack_body(ids_in, num_in, tok_ref, cot_ref, out_ref, ids_ref, num_ref, sems):
    copies = [
        pltpu.make_async_copy(cot_ref, out_ref.at[:TOK], sems.at[0]),
        pltpu.make_async_copy(tok_ref, out_ref.at[TOK_AT:], sems.at[1]),
        pltpu.make_async_copy(ids_in, ids_ref, sems.at[2]),
        pltpu.make_async_copy(num_in, num_ref, sems.at[3]),
    ]
    for copy in copies:
        copy.start()
    copies[2].wait()
    copies[3].wait()
    expert = lax.broadcasted_iota(jnp.int32, (EXPERTS, TOK), 0)
    table = jnp.zeros((EXPERTS, TOK), F32)
    for k in range(TOP):
        weight = num_ref[k : k + 1, :].astype(F32) / DENOM
        table = table + jnp.where(expert == ids_ref[k : k + 1, :], weight, 0.0)
    table = table.astype(BF16)
    out_ref[MARK_AT:TOK_AT, :TILE] = table[:MARK]
    out_ref[MARK_AT:TOK_AT, TILE : 2 * TILE] = table[MARK:]
    out_ref[MARK_AT:TOK_AT, 2 * TILE :] = jnp.zeros((MARK, D - 2 * TILE), BF16)
    for copy in copies[:2]:
        copy.wait()


def plan(at_ref, marks, target_ref, weight_ref):
    n = len(marks) // 2
    core, pos_x, pos_z = at_ref[0], at_ref[1], at_ref[2]
    before = (
        lax.broadcasted_iota(jnp.int32, (TOK, TOK), 0) < lax.broadcasted_iota(jnp.int32, (TOK, TOK), 1)
    ).astype(BF16)
    rows = lax.broadcasted_iota(jnp.int32, (EXPERTS, TOK), 0)
    for d in range(n):
        for g in range(2):
            table = marks[g * n + d]
            routes = jnp.concatenate([table[:, :TILE], table[:, TILE:]], axis=0).astype(F32)
            marked = routes > 0.0
            rank = dot(marked.astype(BF16), before, NN)
            rank = jnp.where(marked, rank + g * SLOTS, -1024.0)
            for s in range(2):
                expert = lax.rem(pos_x + 2 * core + s, X) * Z + pos_z
                mine = rows == expert
                row = jnp.sum(jnp.where(mine, rank, 0.0), axis=0, keepdims=True)
                wt = jnp.sum(jnp.where(mine, routes, 0.0), axis=0, keepdims=True)
                line, cols = d * 2 + s, slice(g * TOK, (g + 1) * TOK)
                target_ref[line : line + 1, cols] = row.astype(jnp.int32) + s * PAIR
                weight_ref[line : line + 1, cols] = wt


def one_hot(target_ref, weight_ref, d, weighted):
    slot = lax.broadcasted_iota(jnp.int32, (2 * PAIR, 2 * TOK), 0)
    first = slot == target_ref[2 * d : 2 * d + 1, :]
    second = slot == target_ref[2 * d + 1 : 2 * d + 2, :]
    if weighted:
        w0 = jnp.broadcast_to(weight_ref[2 * d : 2 * d + 1, :], slot.shape)
        w1 = jnp.broadcast_to(weight_ref[2 * d + 1 : 2 * d + 2, :], slot.shape)
        return jnp.where(first, w0, jnp.where(second, w1, 0.0)).astype(BF16)
    return (first | second).astype(F32).astype(BF16)


def collect(values, target_ref, weight_ref, rows_ref, weighted):
    n = len(values) // 2
    for d in range(n):
        hot = one_hot(target_ref, weight_ref, d, weighted)
        both = jnp.concatenate([values[d], values[n + d]], axis=0)
        got = dot(hot, both, NN).astype(BF16)
        rows_ref[0, d * PAIR : (d + 1) * PAIR, :] = got[:PAIR]
        rows_ref[1, d * PAIR : (d + 1) * PAIR, :] = got[PAIR:]


def spread(rows_ref, target_ref, weight_ref, own_ref, oth_refs, groups, weighted):
    at = slice(0, TOK) if weighted else slice(TOK, 2 * TOK)
    d = 0
    for group, ref in zip(groups, oth_refs):
        for i in range(group):
            hot = one_hot(target_ref, weight_ref, d, weighted)
            both = jnp.concatenate(
                [rows_ref[0, d * PAIR : (d + 1) * PAIR, :], rows_ref[1, d * PAIR : (d + 1) * PAIR, :]], axis=0
            )
            total = dot(hot, both, TN).astype(BF16)
            own_ref[d, at, :] = total[:TOK]
            ref[i, at, :] = total[TOK:]
            d += 1


def expert_body(groups, split, *refs):
    n = sum(groups)
    at_ref, refs = refs[0], list(refs[1:])
    toks, cots, marks = [], [], []
    for _ in range(2):
        for d in range(n):
            if split and d == 0:
                part_t, part_c = refs.pop(0), refs.pop(0)
                marks.append(part_t[:MARK, : 2 * TILE])
                toks.append(part_t[MARK:, :])
                cots.append(part_c[...])
            else:
                ref = refs.pop(0)
                marks.append(ref[MARK_AT:TOK_AT, : 2 * TILE])
                toks.append(ref[TOK_AT:, :])
                cots.append(ref[:TOK, :])
    w0, w1, d0, d1, own_ref = refs[:5]
    oth_refs, refs = refs[5 : 5 + len(groups)], refs[5 + len(groups) :]
    x_ref, c_ref, h_ref, gu_ref, out_rows, grad_rows, target_ref, weight_ref = refs
    plan(at_ref, marks, target_ref, weight_ref)
    collect(toks, target_ref, weight_ref, x_ref, False)
    collect(cots, target_ref, weight_ref, c_ref, True)
    for s, (w, dn) in enumerate(((w0, d0), (w1, d1))):
        rows = x_ref[s]
        both = dot(rows, w[0], NN)
        pre_gate, pre_up = both[:, :FF], both[:, FF:]
        sg = jax.nn.sigmoid(pre_gate)
        silu = pre_gate * sg
        hidden = (silu * pre_up).astype(BF16)
        h_ref[s] = hidden
        out_rows[s] = dot(hidden, dn[0], NN).astype(BF16)
        hidden_grad = dot(c_ref[s], dn[0], NT)
        gate_grad = (hidden_grad * pre_up * sg * (1.0 + pre_gate * (1.0 - sg))).astype(BF16)
        up_grad = (hidden_grad * silu).astype(BF16)
        gu_ref[s, :, :FF] = gate_grad
        gu_ref[s, :, FF:] = up_grad
        grad_rows[s] = dot(gu_ref[s], w[0], NT).astype(BF16)
    spread(out_rows, target_ref, weight_ref, own_ref, oth_refs, groups, True)
    spread(grad_rows, target_ref, weight_ref, own_ref, oth_refs, groups, False)


def experts(at, blocks, weights, groups, split, name):
    n = sum(groups)
    shape = jax.ShapeDtypeStruct
    rows_d, rows_h = shape((2, n * PAIR, D), BF16), shape((2, n * PAIR, FF), BF16)
    mults = 2 * n * PAIR * D * FF * 2
    own, *rest = call(
        functools.partial(expert_body, groups, split),
        (
            shape((n, 2 * TOK, D), BF16),
            *[shape((group, 2 * TOK, D), BF16) for group in groups],
            rows_d,
            rows_d,
            rows_h,
            shape((2, n * PAIR, 2 * FF), BF16),
        ),
        [
            pltpu.VMEM((2, n * PAIR, D), BF16),
            pltpu.VMEM((2, n * PAIR, D), BF16),
            pltpu.VMEM((2 * n, 2 * TOK), jnp.int32),
            pltpu.VMEM((2 * n, 2 * TOK), F32),
        ],
        6 * mults,
        4 * n * 10**6,
        len(blocks) + 4,
        name,
        8 + n,
        smem=1,
    )(at, *blocks, *weights)
    return own, rest[: len(groups)], rest[len(groups) :]


def weights_body(at_ref, *refs):
    pos_y = at_ref[3]
    parts, (a_ref, b_ref) = (refs[:4], refs[4:8]), refs[8:]

    def put(s, part, first, value):
        rel = lax.rem(part // 2 + Y - pos_y, Y)
        for k in range(3):
            row = first + k * TILE
            tile = value[k].astype(BF16)
            low = max(0, min(TILE, A_ROWS - row))
            if low > 0:
                a_ref[s, rel, part % 2, row : row + low, :] = tile[:low]
            if low < TILE:
                b_ref[rel, s, part % 2, row + low - A_ROWS : row + TILE - A_ROWS, :] = tile[low:]

    for s in range(2):
        for q in range(Y):
            cols = slice(q * 2 * TILE, (q + 1) * 2 * TILE)
            both, down = (
                sum(terms)
                for terms in zip(
                    *[
                        (dot(x_ref[s, :, cols], gu_ref[s], TN), dot(h_ref[s], c_ref[s, :, cols], TN))
                        for x_ref, c_ref, h_ref, gu_ref in parts
                    ]
                )
            )
            gate, up = both[:, :FF], both[:, FF:]
            for c in range(2):
                part = 2 * q + c
                lo = c * TILE
                put(s, part, 0, [gate[lo : lo + TILE, k * TILE : (k + 1) * TILE] for k in range(3)])
                put(s, part, 3 * TILE, [up[lo : lo + TILE, k * TILE : (k + 1) * TILE] for k in range(3)])
                put(s, part, 6 * TILE, [down[k * TILE : (k + 1) * TILE, lo : lo + TILE] for k in range(3)])


def add(*values):
    total = values[0].astype(F32)
    for value in values[1:]:
        total = total + value.astype(F32)
    return total.astype(BF16)


def tie(*values):
    return lax.optimization_barrier(values)


def tie(*values):
    return lax.optimization_barrier(values)


def gather(at, block, weights):
    def near(w):
        return move(w, lambda y, c, x, z: (y, c, x - 1, z) if c == 0 else (y, c, x + 1, z))

    def far_down(w):
        return move(w, lambda y, c, x, z: (y, 1, x - 1, z) if c == 0 else (y, 0, x, z))

    def far_up(w):
        return move(w, lambda y, c, x, z: (y, 1, x + 1, z) if c == 1 else (y, 0, x, z))

    gate, up, down = weights
    right, left, gate_n, up_n, oth0 = tie(z_right(block), z_left(block), near(gate), near(up), swap(block))
    own, oth = {0: block, 7: right, 1: left}, {0: oth0}
    right, left, gate_f, up_f, down_n = tie(
        z_right(right), z_left(left), far_down(gate_n), far_up(up_n), near(down)
    )
    own[6], own[2] = right, left
    core = lax.axis_index("c")
    wide_s = jnp.where(core == 0, jnp.concatenate([gate, up], axis=2), jnp.concatenate([gate_f, up_f], axis=2))
    wide_n = jnp.concatenate([gate_n, up_n], axis=2)
    oth[6], oth[2] = swap(own[6]), swap(own[2])
    right, left, down_f, oth[7], oth[1], wide_s, wide_n = tie(
        z_right(right), z_left(left), far_down(down_n), swap(own[7]), swap(own[1]), wide_s, wide_n
    )
    own[5], own[3] = right, left
    full = [wide_s, wide_n, jnp.where(core == 0, down, down_f), down_n]
    spots = [2, 6, 1, 7, 0]
    near_work = experts(at, [own[d] for d in spots] + [oth[d] for d in spots], full, (2, 2, 1), False, "near")
    near_own, near_oth, near_rows = near_work
    far_t, far_c, oth[5], oth[3], near_own = tie(
        z_right(right[TOK:]), z_left(left[:TOK]), swap(right), swap(left), near_own
    )
    near_work = near_own, near_oth, near_rows
    far_work = experts(
        at,
        [far_t, far_c, own[3], own[5], swap(far_t), swap(far_c), oth[3], oth[5]],
        full,
        (1, 2),
        True,
        "far",
    )
    return near_work, far_work


def padded(got, first):
    zero = jnp.zeros((TOK, D), BF16)
    return jnp.concatenate([got, zero] if first else [zero, got], axis=0)


def x_merge(v):
    return move(v, lambda y, c, x, z: (y, 0, x + 1, z) if c == 0 else (y, 1, x - 1, z))


def pick(v, core, axis):
    first, second = (lax.index_in_dim(v, i, axis, keepdims=False) for i in range(2))
    return jnp.where(core == 0, first, second), jnp.where(core == 0, second, first)


def x_cross(v):
    return move(v, lambda y, c, x, z: (y, 1, x + 1, z) if c == 0 else (y, 0, x - 1, z))


def first_half(v, core):
    first, second = v
    (got,) = yield [(x_one, first)]
    three = got[:, 1]
    second = add(second, jnp.where(core == 0, got, jnp.zeros_like(got)))
    mine, other = pick(second, core, 1)
    keep, _ = pick(first, core, 1)
    one, two = yield [(x_merge, mine), (x_cross, other)]
    v = add(jnp.where(core == 0, keep, three), one, two)
    one, two, three = yield [(y_right, v[1]), (y_two, v[2]), (y_left, v[3])]
    return add(v[0], one, two, three)


def second_half(v, core):
    got, right = yield [(y_left, v[2]), (y_right, v[1])]
    (left,) = yield [(y_left, add(v[3], got))]
    first, second = add(v[0], right, left)
    got, two = yield [(x_merge, second), (x_two, first)]
    zero = jnp.zeros_like(first)
    v = add(got, jnp.where(core == 0, first, zero), jnp.where(core == 0, two, zero))
    keep, send = pick(v, core, 0)
    (got,) = yield [(swap, send)]
    return add(keep, got)


def x_one(v):
    return move(v, lambda y, c, x, z: (y, 0, x + 1, z) if c == 1 else (y, 1, x, z))


def x_two(v):
    return move(v, lambda y, c, x, z: (y, 0, x + 2, z) if c == 1 else (y, 1, x, z))


def y_two(v):
    return move(v, lambda y, c, x, z: (y + 2, c, x, z))


def local(tokens, expert_ids, route_num, w_gate, w_up, w_down, cotangent):
    core = lax.axis_index("c")
    at = jnp.stack([core, lax.axis_index("x"), lax.axis_index("z"), lax.axis_index("y")]).astype(jnp.int32)
    shape = jax.ShapeDtypeStruct
    table = [pltpu.VMEM((TOP, TOK), jnp.int32), pltpu.VMEM((TOP, TOK), jnp.int32), pltpu.SemaphoreType.DMA((4,))]
    block = call(pack_body, shape((BLOCK, D), BF16), table, 10**6, 2 * 10**6, 0, "pack", 4, n_hbm=4)(
        expert_ids.T, route_num.T, tokens, cotangent
    )
    near_work, far_work = gather(at, block, [w_gate, w_up, w_down])
    mults = 2 * ROWS * D * FF * 2
    own = dict(zip((4, 3, 5), far_work[0])) | dict(zip((2, 6, 1, 7, 0), near_work[0]))
    oth = far_work[1] + near_work[1]
    far_rows = list(far_work[2])
    near, far_rows[0] = tie(swap(oth[0]), far_rows[0])
    near = near[0]
    right, left = z_right(add(own[4][:TOK], near[:TOK])), z_left(add(own[4][TOK:], near[TOK:]))
    others = [swap(v) for v in oth[1:]]
    parts_a, parts_b = shape((2, Y, 2, A_ROWS, TILE), BF16), shape((Y, 2, 2, B_ROWS, TILE), BF16)
    part_a, part_b = call(weights_body, (parts_a, parts_b), [], 3 * mults, 15 * 10**6, 8, "weights", 12, smem=1)(
        at, *near_work[2], *far_rows
    )
    right, left, part_b, *others = tie(right, left, part_b, *others)

    def finish(work):
        step = next(work)
        while True:
            try:
                step = work.send(tuple(fn(value) for fn, value in step))
            except StopIteration as stop:
                return stop.value

    sum_a, sum_b = finish(first_half(part_a, core)), finish(second_half(part_b, core))
    right, left = padded(right, True), padded(left, False)
    for k in (3, 2, 1):
        near = others.pop(0)
        right, left = add(own[k], near[0], right), add(own[Z - k], near[1], left)
        right, left = tie(z_right(right), z_left(left))
    last = [own[0], others[0][0], right, left]
    output, tokens_grad = add(*[v[:TOK] for v in last]), add(*[v[TOK:] for v in last])
    total = jnp.concatenate([sum_a.reshape(A_ROWS, TILE), sum_b.reshape(B_ROWS, TILE)], axis=0).reshape(3, 3, TILE, TILE)
    wide = lambda v: jnp.concatenate([v[0], v[1], v[2]], axis=1)[None]
    return output, tokens_grad, wide(total[0]), wide(total[1]), total[2].reshape(1, FF, TILE)


def solution(mesh):
    grid = Mesh(mesh.devices.reshape(Y, C, X, Z), AXES)
    rows = P(AXES, None)
    expert = P(("x", "z"), None, None)
    in_specs = (rows, rows, rows, expert, expert, expert, rows)
    out_specs = (
        rows,
        rows,
        P(("x", "z"), ("y", "c"), None),
        P(("x", "z"), ("y", "c"), None),
        P(("x", "z"), None, ("y", "c")),
    )
    return jax.shard_map(local, mesh=grid, in_specs=in_specs, out_specs=out_specs, check_vma=False)
```
